32 devices in a mesh: series: 2 (over x), tm: 16 (over z, y, core).
Axes of the slice: x: 2, y: 2, z: 4, core: 2. Of those that a mesh axis runs over, the one named last changes fastest.
Arguments:
- y_obs: bfloat16 [8192, 8192], P('series', 'tm'), may hold values from -6 to 6
- tile_mask: int32 [64, 64], P('series', 'tm'), may hold values 0 or 1
- factors: float32 [8192, 128], P(('series', 'tm')), may hold values from -0.5 to 0.5
- adam_m: float32 [8192, 128], P(('series', 'tm')), may hold values from -3 to 3
- adam_v: float32 [8192, 128], P(('series', 'tm')), may hold values from 0.1 to 10
- basis: float32 [128, 8192], P('series', 'tm'), may hold values from -6 to 6
- dilations: int32 [4], replicated, may hold values from 1 to 32, as said below
- conv_w: bfloat16 [4, 2, 128, 128], replicated, may hold values from -0.375 to 0.375
- conv_b: float32 [4, 128], replicated, may hold values from -3 to 3
Outputs:
- factors_new: float32 [8192, 128], P(('series', 'tm'))
- m_new: float32 [8192, 128], P(('series', 'tm'))
- v_new: float32 [8192, 128], P(('series', 'tm'))
- basis_new: float32 [128, 8192], P('series', 'tm')
The draws below stay inside these ranges and needn't reach their ends.
Inputs may be any that keep to these rules, and one draw needn't show every extreme that they name: `dilations`: at least one layer has dilation 32.
All inputs are finite; a program needn't handle non-finite values. No bound on the sum of `tile_mask` on one device may be relied on, other than what follows from the above.
Results may differ from the reference program's by a relative error of at most 0.0031.
Values may be sent and summed in bfloat16 or wider, within the bound.
A program may use at most 64 MiB of HBM per device.

```python
import math
import jax
import jax.numpy as jnp
from jax import lax

K = 128
TILE = 128
LAYERS = 4
D_MAX = 32
NS = 8192
NT = 8192


def draw_dilations(key, part):
    first, second = jax.random.split(jax.random.fold_in(key, 17))
    values = jax.random.randint(first, (LAYERS,), 1, D_MAX + 1).astype(jnp.int32)
    where_top = jax.random.randint(second, (), 0, LAYERS)
    return values.at[where_top].set(D_MAX).astype(jnp.int32)


def set_ends(entries, key, smallest, top_value):
    dims = entries.shape
    place = [jax.random.randint(jax.random.fold_in(key, axis), (), 0, dims[axis]) for axis in range(len(dims))]
    entries = entries.at[tuple(place)].set(smallest)
    longest = dims.index(max(dims))
    place[longest] = (place[longest] + 1) % dims[longest]
    return entries.at[tuple(place)].set(top_value)


def steps_of(key, dims, cuts, least, top_value):
    def one(position, shards_of):
        steps = jax.random.uniform(jax.random.fold_in(jax.random.fold_in(key, 6), position), (shards_of,), jnp.float32, least / len(cuts), top_value / len(cuts))
        return jnp.repeat(jnp.exp(steps), dims[position] // shards_of).reshape((-1,) + (1,) * (len(dims) - position - 1))

    level = one(*cuts[0])
    for cut in cuts[1:]:
        level = level * one(*cut)
    return level


def noise(rng, extent, scale, reach, cuts=(), dtype=jnp.bfloat16):
    values = scale * jax.random.normal(rng, extent, jnp.float32)
    if cuts:
        values = values * steps_of(rng, extent, cuts, -0.22, 0.18)
    return jnp.clip(values, -reach, reach).astype(dtype)


def setup_inputs(seed: int = 0) -> dict:
    streams_of = jax.random.split(jax.random.key(seed), 10)
    y_obs = noise(streams_of[0], (NS, NT), 1.0, 6.0, ((0, 2), (1, 16)))
    tile_mask = set_ends((jax.random.randint(streams_of[1], (NS // TILE, NT // TILE), 0, 4) < 3).astype(jnp.int32), jax.random.fold_in(streams_of[1], 1), 0, 1)
    factors = noise(streams_of[2], (NS, K), K ** -0.5, 0.5, ((0, 32),), jnp.float32)
    adam_m = noise(streams_of[3], (NS, K), 0.5, 3.0, ((0, 32),), jnp.float32)
    adam_v = jnp.clip(jnp.exp(math.log(10.0) - 4.6051702 * jax.random.uniform(streams_of[4], (NS, K), jnp.float32) ** steps_of(streams_of[4], (NS, K), ((0, 32),), -0.2, 0.2)), 0.1, 10.0)
    basis = noise(streams_of[5], (K, NT), 1.0, 6.0, ((0, 2), (1, 16)), jnp.float32)
    dilations = draw_dilations(jax.random.fold_in(streams_of[9], 71), 0)
    conv_w = noise(streams_of[7], (LAYERS, 2, K, K), (2 * K) ** -0.5, 0.375)
    conv_b = noise(streams_of[8], (LAYERS, K), 0.5, 3.0, (), jnp.float32)
    return dict(y_obs=y_obs, tile_mask=tile_mask, factors=factors, adam_m=adam_m, adam_v=adam_v, basis=basis, dilations=dilations, conv_w=conv_w, conv_b=conv_b)


def expand(tiles, tile):
    rows, cols = tiles.shape
    ones = tiles.astype(jnp.float32)
    return jnp.broadcast_to(ones[:, None, :, None], (rows, tile, cols, tile)).reshape(rows * tile, cols * tile)

def adam_update(factors, adam_m, adam_v, grad_f):
    m_new = 0.9 * adam_m + 0.1 * grad_f
    v_new = 0.999 * adam_v + 0.001 * grad_f * grad_f
    m_hat = m_new / (1.0 - 0.9 ** 10)
    v_hat = v_new / (1.0 - 0.999 ** 10)
    return (factors - 0.01 * m_hat / (jnp.sqrt(v_hat) + 1e-08), m_new, v_new)

def reference(y_obs, tile_mask, factors, adam_m, adam_v, basis, dilations, conv_w, conv_b):
    xb = basis.astype(jnp.bfloat16)
    block = math.gcd(NS, 1024)
    count = NS // block
    y_blocks = y_obs.reshape(count, block, NT)
    m_blocks = tile_mask.reshape(count, block // TILE, NT // TILE)
    f_blocks = factors.astype(jnp.bfloat16).reshape(count, block, K)
    scale_f = 1.0 / math.sqrt(NT)

    def sweep(total, item):
        y_part, m_part, f_part = item
        pred = jnp.dot(f_part, xb, preferred_element_type=jnp.float32)
        resid = expand(m_part, TILE) * (y_part.astype(jnp.float32) - pred)
        rb = resid.astype(jnp.bfloat16)
        grad_part = -lax.dot_general(rb, xb, (((1,), (1,)), ((), ())), preferred_element_type=jnp.float32) * scale_f
        total = total - lax.dot_general(f_part, rb, (((0,), (0,)), ((), ())), preferred_element_type=jnp.float32)
        return (total, grad_part)
    total, grads = lax.scan(sweep, jnp.zeros((K, NT), jnp.float32), (y_blocks, m_blocks, f_blocks))
    grad_f = grads.reshape(NS, K)
    grad_x = total * math.sqrt(K / NS)
    factors_new, m_new, v_new = adam_update(factors, adam_m, adam_v, grad_f)
    hidden = xb.astype(jnp.float32)
    for layer in range(LAYERS):
        hb = hidden.astype(jnp.bfloat16)
        padded = jnp.concatenate([jnp.zeros((K, D_MAX), jnp.bfloat16), hb], axis=1)
        past = lax.dynamic_slice_in_dim(padded, (D_MAX - dilations[layer]).astype(jnp.int32), NT, 1)
        z_val = jnp.dot(conv_w[layer, 0], past, preferred_element_type=jnp.float32)
        z_val = z_val + jnp.dot(conv_w[layer, 1], hb, preferred_element_type=jnp.float32)
        z_val = z_val + conv_b[layer][:, None]
        hidden = hidden + jax.nn.relu(z_val)
    basis_new = basis - 0.5 * (grad_x + (basis - hidden))
    return (factors_new, m_new, v_new, basis_new)
```

```python
import functools
import math

import jax
import jax.numpy as jnp
from jax import lax
from jax.experimental import pallas as pl
from jax.experimental.pallas import tpu as pltpu
from jax.sharding import PartitionSpec as P

K = 128
TILE = 128
LAYERS = 4
D_MAX = 32
REACH = LAYERS * D_MAX
MESH = pl.DeviceIdType.MESH
F32 = jnp.float32
BF16 = jnp.bfloat16


def kernel(
    count,
    groups,
    y_hbm,
    mask_ref,
    f_hbm,
    m_hbm,
    v_hbm,
    b_hbm,
    dil_ref,
    w_hbm,
    cb_hbm,
    f_out,
    m_out,
    v_out,
    b_out,
    y_buf,
    f_own,
    m_own,
    v_own,
    b_own,
    w_buf,
    cb_buf,
    f_buf,
    x_buf,
    xt_buf,
    rim,
    g_own,
    g_give,
    g_take,
    sum_out,
    sum_in,
    gx,
    gx_out,
    gx_in,
    h_buf,
    load_sem,
    ring_send,
    ring_recv,
    pair_send,
    pair_recv,
    x_send,
    x_recv,
    rim_sem,
    give_send,
    give_recv,
    sum_send,
    sum_recv,
    gx_send,
    gx_recv,
):
    chips = count // 2
    far = chips // 2
    side = count // 4
    rows = f_own.shape[0]
    piece = rows // 2
    part, width = b_own.shape
    total_time = width * count
    total_series = rows * count * groups

    series = lax.axis_index("series")
    tm = lax.axis_index("tm")
    core = lax.rem(tm, 2)
    twin = 1 - core
    chip = tm // 2
    z_at, y_at = chip // 2, lax.rem(chip, 2)
    here = z_at + y_at * (2 * side - 1 - 2 * z_at)

    def at(offset):
        return lax.rem(here + offset + chips, chips)

    def chip_of(position):
        back = position // side
        return 2 * (position + back * (2 * side - 1 - 2 * position)) + back

    def member(position, which):
        return (series, 2 * chip_of(position) + which)

    after, before = member(at(1), core), member(at(-1), core)
    sibling = (series, tm + 1 - 2 * core)
    following = (series, lax.rem(tm + 1, count))
    preceding = (series, lax.rem(tm + count - 1, count))

    loads = [
        pltpu.make_async_copy(source, target, load_sem.at[index])
        for index, (source, target) in enumerate(
            (
                (b_hbm, b_own),
                (f_hbm, f_own),
                (y_hbm, y_buf),
                (w_hbm, w_buf),
                (cb_hbm, cb_buf),
                (m_hbm, m_own),
                (v_hbm, v_own),
            )
        )
    ]
    for load in loads:
        load.start()

    barrier = pltpu.get_barrier_semaphore()
    others = [(lax.rem(series + step, groups), tm) for step in range(1, groups)]
    greeted = [after, before, sibling, following, preceding] + others
    for device in greeted:
        pl.semaphore_signal(barrier, inc=1, device_id=device, device_id_type=MESH)
    loads[1].wait()
    f_buf[here, core] = f_own[...].astype(BF16)
    loads[0].wait()
    x_buf[series] = b_own[...].astype(BF16)
    gx[...] = jnp.zeros_like(gx)
    pl.semaphore_wait(barrier, len(greeted))

    def remote(source, target, send, recv, device):
        return pltpu.make_async_remote_copy(
            src_ref=source,
            dst_ref=target,
            send_sem=send,
            recv_sem=recv,
            device_id=device,
            device_id_type=MESH,
        )

    pending = []

    def send(copy):
        copy.start()
        pending.append(copy)

    def ring_copy(way, step, half):
        position = at(-(step - 1) if way == 0 else step - 1)
        ref = f_buf.at[position, core, pl.ds(half * piece, piece)]
        index = (way, step - 1, half)
        return remote(
            ref, ref, ring_send.at[index], ring_recv.at[index], after if way == 0 else before
        )

    def ring_arrival(way, step, half):
        position = at(-step if way == 0 else step)
        ref = f_buf.at[position, core, pl.ds(half * piece, piece)]
        index = (way, step - 1, half)
        return remote(
            ref, ref, ring_send.at[index], ring_recv.at[index], after if way == 0 else before
        )

    def pair_copy(position, half, which):
        ref = f_buf.at[position, which, pl.ds(half * piece, piece)]
        return remote(
            ref, ref, pair_send.at[position, half], pair_recv.at[position, half], sibling
        )

    def travels(way, step, half):
        return step < far or (step == far and half == way)

    for half in range(2):
        for way in range(2):
            if travels(way, 1, half):
                send(ring_copy(way, 1, half))
    for step in range(1, groups):
        send(
            remote(
                x_buf.at[series],
                x_buf.at[series],
                x_send.at[step - 1],
                x_recv.at[step - 1],
                others[step - 1],
            )
        )
    for half in range(2):
        send(pair_copy(here, half, core))

    for step in range(1, groups):
        origin = lax.rem(series + groups - step, groups)
        remote(
            x_buf.at[origin],
            x_buf.at[origin],
            x_send.at[step - 1],
            x_recv.at[step - 1],
            others[step - 1],
        ).wait_recv()
    rim_copy = remote(
        x_buf.at[:, :, pl.ds(width - REACH, REACH)],
        rim,
        rim_sem.at[0],
        rim_sem.at[1],
        following,
    )
    send(rim_copy)
    x_now = x_buf[...].reshape(K, width)
    xt_buf[...] = x_now.astype(F32).T.astype(BF16)
    loads[2].wait()

    band = min(rows, TILE)

    def compute(position, which):
        block = 2 * chip_of(position) + which
        f_now = f_buf[position, which]
        x_full = x_buf[...].reshape(K, width)
        pred = jnp.dot(f_now, x_full, preferred_element_type=F32)
        parts = []
        for index in range(rows // band):
            start = pl.multiple_of(block * rows + index * band, band)
            tile_row = start // TILE
            y_now = y_buf[pl.ds(start, band), :].astype(F32)
            seen = jnp.concatenate(
                [
                    jnp.full((1, TILE), mask_ref[tile_row, column].astype(F32))
                    for column in range(width // TILE)
                ],
                axis=1,
            )
            inner = pred[index * band : (index + 1) * band]
            parts.append((seen * (y_now - inner)).astype(BF16))
        rb = jnp.concatenate(parts, axis=0) if len(parts) > 1 else parts[0]
        gx[...] += lax.dot_general(
            f_now, rb, (((0,), (0,)), ((), ())), preferred_element_type=F32
        )
        return jnp.dot(rb, xt_buf[...], preferred_element_type=F32)

    def give_copy(position):
        return remote(
            g_give.at[position],
            g_take.at[position],
            give_send.at[position],
            give_recv.at[position],
            sibling,
        )

    def compute_own(position):
        g_own[position] = compute(position, core)

    def compute_twin(position):
        for half in range(2):
            pair_copy(position, half, twin).wait_recv()
        g_give[position] = compute(position, twin).astype(BF16)
        give_copy(position).start()

    def both_ways(step, work):
        if step == 0:
            work(here)
            return

        @pl.loop(0, 2)
        def _(way):
            work(lax.rem(here + chips + (2 * way - 1) * step, chips))

    for step in range(1, far + 1):
        for half in range(2):
            for way in range(2):
                if travels(way, step, half):
                    ring_arrival(way, step, half).wait_recv()
                    if travels(way, step + 1, half):
                        send(ring_copy(way, step + 1, half))
                    send(pair_copy(at(-step if way == 0 else step), half, core))
            both_ways(step - 1, compute_own if half == 1 else compute_twin)

    def total_of(position, half):
        rows_of = pl.ds(half * piece, piece)
        return g_own[position, rows_of] + g_take[position, rows_of].astype(F32)

    def sum_copy(way, step, half):
        index = (way, step - 1, half)
        return remote(
            sum_out.at[index],
            sum_in.at[index],
            sum_send.at[index],
            sum_recv.at[index],
            after if way == 0 else before,
        )

    def send_sum(way, step, half):
        value = total_of(at(step if way == 0 else -step), half)
        if travels(way, step + 1, half):
            sum_copy(way, step + 1, half).wait_recv()
            value = value + sum_in[way, step, half].astype(F32)
        sum_out[way, step - 1, half] = value.astype(BF16)
        send(sum_copy(way, step, half))

    compute_twin(at(far))
    for step in (far - 1, 1 - far):
        give_copy(at(step)).wait_recv()
    for way in range(2):
        send_sum(way, far - 1, 1 - way)
    compute_own(at(far))

    for step in range(1, groups):
        target = lax.rem(series + step, groups)
        rows_of = pl.ds(pl.multiple_of(target * part, part), part)
        gx_out[step - 1] = gx[rows_of, :].astype(BF16)
        send(
            remote(
                gx_out.at[step - 1],
                gx_in.at[step - 1],
                gx_send.at[step - 1],
                gx_recv.at[step - 1],
                others[step - 1],
            )
        )

    give_copy(at(far)).wait_recv()
    for way in range(2):
        send_sum(way, far, way)

    span = width + REACH
    rim_copy.wait_recv()
    loads[3].wait()
    loads[4].wait()
    places = tm * width - REACH + lax.broadcasted_iota(jnp.int32, (K, span), 1)
    inside = places >= 0
    hidden = jnp.concatenate([rim[...].reshape(K, REACH), x_now], axis=1).astype(F32)
    hidden = jnp.where(inside, hidden, 0.0)

    def conv_layer(hidden, layer):
        hb = hidden.astype(BF16)
        past = pltpu.roll(hb.astype(F32), dil_ref[layer], 1).astype(BF16)
        z_val = jnp.dot(w_buf[layer, 0], past, preferred_element_type=F32)
        z_val = z_val + jnp.dot(w_buf[layer, 1], hb, preferred_element_type=F32)
        z_val = z_val + cb_buf[layer][:, None]
        return jnp.where(inside, hidden + jnp.maximum(z_val, 0.0), 0.0)

    layer = 0
    for step in range(far - 1, 0, -1):
        if layer < LAYERS:
            hidden = conv_layer(hidden, layer)
            layer += 1
        if step < far - 1:
            for offset in (step, -step):
                give_copy(at(offset)).wait_recv()
        for half in range(2):
            for way in range(2):
                if step < far - 1 or half == way:
                    send_sum(way, step, half)
    while layer < LAYERS:
        hidden = conv_layer(hidden, layer)
        layer += 1
    h_buf[...] = hidden[:, REACH:]

    own_rows = pl.ds(pl.multiple_of(series * part, part), part)
    grad_x = gx[own_rows, :]
    for step in range(1, groups):
        remote(
            gx_out.at[step - 1],
            gx_in.at[step - 1],
            gx_send.at[step - 1],
            gx_recv.at[step - 1],
            others[step - 1],
        ).wait_recv()
        grad_x = grad_x + gx_in[step - 1].astype(F32)
    grad_x = -grad_x * math.sqrt(K / total_series)
    basis = b_own[...]
    b_out[...] = basis - 0.5 * (grad_x + (basis - h_buf[own_rows, :]))

    loads[5].wait()
    loads[6].wait()
    give_copy(here).wait_recv()
    scale_f = 1.0 / math.sqrt(total_time)
    for half in range(2):
        rows_of = pl.ds(half * piece, piece)
        value = total_of(here, half)
        for way in range(2):
            sum_copy(way, 1, half).wait_recv()
            value = value + sum_in[way, 0, half].astype(F32)
        grad_f = -value * scale_f
        m_new = 0.9 * m_own[rows_of] + 0.1 * grad_f
        v_new = 0.999 * v_own[rows_of] + 0.001 * grad_f * grad_f
        m_hat = m_new / (1.0 - 0.9**10)
        v_hat = v_new / (1.0 - 0.999**10)
        f_out[rows_of] = f_own[rows_of] - 0.01 * m_hat / (jnp.sqrt(v_hat) + 1e-08)
        m_out[rows_of] = m_new
        v_out[rows_of] = v_new

    for copy in pending:
        copy.wait_send()

    @pl.loop(0, chips)
    def _(position):
        give_copy(position).wait_send()


def on_device(count, groups, y_obs, tile_mask, factors, adam_m, adam_v, basis, dilations, conv_w, conv_b):
    rows = factors.shape[0]
    part, width = basis.shape
    chips = count // 2
    far = chips // 2
    piece = rows // 2
    dma = pltpu.SemaphoreType.DMA
    hbm = pl.BlockSpec(memory_space=pl.ANY)
    smem = pl.BlockSpec(memory_space=pltpu.SMEM)
    vmem = pl.BlockSpec(memory_space=pltpu.VMEM)
    work = y_obs.shape[0] * width * K * 6
    return pl.pallas_call(
        functools.partial(kernel, count, groups),
        out_shape=(
            jax.ShapeDtypeStruct(factors.shape, F32),
            jax.ShapeDtypeStruct(factors.shape, F32),
            jax.ShapeDtypeStruct(factors.shape, F32),
            jax.ShapeDtypeStruct(basis.shape, F32),
        ),
        in_specs=[hbm, smem, hbm, hbm, hbm, hbm, smem, hbm, hbm],
        out_specs=(vmem, vmem, vmem, vmem),
        scratch_shapes=[
            pltpu.VMEM(y_obs.shape, BF16),
            pltpu.VMEM(factors.shape, F32),
            pltpu.VMEM(factors.shape, F32),
            pltpu.VMEM(factors.shape, F32),
            pltpu.VMEM(basis.shape, F32),
            pltpu.VMEM(conv_w.shape, BF16),
            pltpu.VMEM(conv_b.shape, F32),
            pltpu.VMEM((chips, 2, rows, K), BF16),
            pltpu.VMEM((groups, part, width), BF16),
            pltpu.VMEM((width, K), BF16),
            pltpu.VMEM((groups, part, REACH), BF16),
            pltpu.VMEM((chips, rows, K), F32),
            pltpu.VMEM((chips, rows, K), BF16),
            pltpu.VMEM((chips, rows, K), BF16),
            pltpu.VMEM((2, far, 2, piece, K), BF16),
            pltpu.VMEM((2, far, 2, piece, K), BF16),
            pltpu.VMEM((K, width), F32),
            pltpu.VMEM((max(groups - 1, 1), part, width), BF16),
            pltpu.VMEM((max(groups - 1, 1), part, width), BF16),
            pltpu.VMEM((K, width), F32),
            dma((7,)),
            dma((2, far, 2)),
            dma((2, far, 2)),
            dma((chips, 2)),
            dma((chips, 2)),
            dma((max(groups - 1, 1),)),
            dma((max(groups - 1, 1),)),
            dma((2,)),
            dma((chips,)),
            dma((chips,)),
            dma((2, far, 2)),
            dma((2, far, 2)),
            dma((max(groups - 1, 1),)),
            dma((max(groups - 1, 1),)),
        ],
        compiler_params=pltpu.CompilerParams(
            collective_id=0, has_side_effects=True, vmem_limit_bytes=40 * 2**20
        ),
        cost_estimate=pl.CostEstimate(
            flops=work, bytes_accessed=2 * y_obs.size, transcendentals=factors.size
        ),
    )(y_obs, tile_mask, factors, adam_m, adam_v, basis, dilations, conv_w, conv_b)


def solution(mesh):
    return jax.shard_map(
        functools.partial(on_device, mesh.shape["tm"], mesh.shape["series"]),
        mesh=mesh,
        in_specs=(
            P("series", "tm"),
            P("series", "tm"),
            P(("series", "tm"), None),
            P(("series", "tm"), None),
            P(("series", "tm"), None),
            P("series", "tm"),
            P(),
            P(),
            P(),
        ),
        out_specs=(
            P(("series", "tm"), None),
            P(("series", "tm"), None),
            P(("series", "tm"), None),
            P("series", "tm"),
        ),
        check_vma=False,
    )
```

```python
import functools
import math

import jax
import jax.numpy as jnp
from jax import lax
from jax.experimental import pallas as pl
from jax.experimental.pallas import tpu as pltpu
from jax.sharding import PartitionSpec as P

K = 128
TILE = 128
LAYERS = 4
D_MAX = 32
REACH = LAYERS * D_MAX
MESH = pl.DeviceIdType.MESH
F32 = jnp.float32
BF16 = jnp.bfloat16


def kernel(
    count,
    groups,
    y_hbm,
    mask_hbm,
    f_hbm,
    m_hbm,
    v_hbm,
    b_hbm,
    dil_hbm,
    w_hbm,
    cb_hbm,
    f_end,
    m_end,
    v_end,
    b_end,
    f_out,
    m_out,
    v_out,
    b_out,
    y_buf,
    mask_in,
    mask_ref,
    dil_ref,
    f_own,
    m_own,
    v_own,
    b_own,
    w_buf,
    cb_buf,
    f_buf,
    x_buf,
    xt_buf,
    rim,
    g_own,
    g_give,
    g_take,
    sum_out,
    sum_in,
    gx,
    gx_out,
    gx_in,
    h_buf,
    load_sem,
    ring_send,
    ring_recv,
    pair_send,
    pair_recv,
    x_send,
    x_recv,
    rim_sem,
    give_send,
    give_recv,
    sum_send,
    sum_recv,
    gx_send,
    gx_recv,
):
    chips = count // 2
    far = chips // 2
    side = count // 4
    rows = f_own.shape[0]
    piece = rows // 2
    part, width = b_own.shape
    total_time = width * count
    total_series = rows * count * groups

    series = lax.axis_index("series")
    tm = lax.axis_index("tm")
    core = lax.rem(tm, 2)
    twin = 1 - core
    chip = tm // 2
    z_at, y_at = chip // 2, lax.rem(chip, 2)
    here = z_at + y_at * (2 * side - 1 - 2 * z_at)

    def at(offset):
        return lax.rem(here + offset + chips, chips)

    def chip_of(position):
        back = position // side
        return 2 * (position + back * (2 * side - 1 - 2 * position)) + back

    def member(position, which):
        return (series, 2 * chip_of(position) + which)

    after, before = member(at(1), core), member(at(-1), core)
    sibling = (series, tm + 1 - 2 * core)
    following = (series, lax.rem(tm + 1, count))
    preceding = (series, lax.rem(tm + count - 1, count))

    loads = [
        pltpu.make_async_copy(source, target, load_sem.at[index])
        for index, (source, target) in enumerate(
            (
                (b_hbm, b_own),
                (f_hbm, f_own),
                (y_hbm, y_buf),
                (w_hbm, w_buf),
                (cb_hbm, cb_buf),
                (m_hbm, m_own),
                (v_hbm, v_own),
                (mask_hbm, mask_in),
                (dil_hbm, dil_ref),
            )
        )
    ]
    for load in loads:
        load.start()

    barrier = pltpu.get_barrier_semaphore()
    others = [(lax.rem(series + step, groups), tm) for step in range(1, groups)]
    greeted = [after, before, sibling, following, preceding] + others
    for device in greeted:
        pl.semaphore_signal(barrier, inc=1, device_id=device, device_id_type=MESH)
    loads[1].wait()
    f_buf[here, core] = f_own[...].astype(BF16)
    loads[0].wait()
    x_buf[series] = b_own[...].astype(BF16)
    gx[...] = jnp.zeros_like(gx)
    pl.semaphore_wait(barrier, len(greeted))

    def remote(source, target, send, recv, device):
        return pltpu.make_async_remote_copy(
            src_ref=source,
            dst_ref=target,
            send_sem=send,
            recv_sem=recv,
            device_id=device,
            device_id_type=MESH,
        )

    pending = []

    def send(copy):
        copy.start()
        pending.append(copy)

    def ring_copy(way, step, half):
        position = at(-(step - 1) if way == 0 else step - 1)
        ref = f_buf.at[position, core, pl.ds(half * piece, piece)]
        index = (way, step - 1, half)
        return remote(
            ref, ref, ring_send.at[index], ring_recv.at[index], after if way == 0 else before
        )

    def ring_arrival(way, step, half):
        position = at(-step if way == 0 else step)
        ref = f_buf.at[position, core, pl.ds(half * piece, piece)]
        index = (way, step - 1, half)
        return remote(
            ref, ref, ring_send.at[index], ring_recv.at[index], after if way == 0 else before
        )

    def pair_copy(position, half, which):
        ref = f_buf.at[position, which, pl.ds(half * piece, piece)]
        return remote(
            ref, ref, pair_send.at[position, half], pair_recv.at[position, half], sibling
        )

    def travels(way, step, half):
        return step < far or (step == far and half == way)

    for half in range(2):
        for way in range(2):
            if travels(way, 1, half):
                send(ring_copy(way, 1, half))
    for step in range(1, groups):
        send(
            remote(
                x_buf.at[series],
                x_buf.at[series],
                x_send.at[step - 1],
                x_recv.at[step - 1],
                others[step - 1],
            )
        )
    for half in range(2):
        send(pair_copy(here, half, core))

    for step in range(1, groups):
        origin = lax.rem(series + groups - step, groups)
        remote(
            x_buf.at[origin],
            x_buf.at[origin],
            x_send.at[step - 1],
            x_recv.at[step - 1],
            others[step - 1],
        ).wait_recv()
    rim_copy = remote(
        x_buf.at[:, :, pl.ds(width - REACH, REACH)],
        rim,
        rim_sem.at[0],
        rim_sem.at[1],
        following,
    )
    send(rim_copy)
    x_now = x_buf[...].reshape(K, width)
    xt_buf[...] = x_now.astype(F32).T.astype(BF16)
    loads[2].wait()
    loads[7].wait()
    mask_ref[...] = mask_in[...].astype(F32).T

    band = min(rows, TILE)

    def compute(position, which):
        block = 2 * chip_of(position) + which
        f_now = f_buf[position, which]
        x_full = x_buf[...].reshape(K, width)
        pred = jnp.dot(f_now, x_full, preferred_element_type=F32)
        parts = []
        for index in range(rows // band):
            start = pl.multiple_of(block * rows + index * band, band)
            tile_row = start // TILE
            y_now = y_buf[pl.ds(start, band), :].astype(F32)
            flags = mask_ref[pl.ds(tile_row, 1), :]
            seen = jnp.concatenate(
                [
                    jnp.broadcast_to(flags[:, column : column + 1], (1, TILE))
                    for column in range(width // TILE)
                ],
                axis=1,
            )
            inner = pred[index * band : (index + 1) * band]
            parts.append((seen * (y_now - inner)).astype(BF16))
        rb = jnp.concatenate(parts, axis=0) if len(parts) > 1 else parts[0]
        gx[...] += lax.dot_general(
            f_now, rb, (((0,), (0,)), ((), ())), preferred_element_type=F32
        )
        return jnp.dot(rb, xt_buf[...], preferred_element_type=F32)

    def give_copy(position):
        return remote(
            g_give.at[position],
            g_take.at[position],
            give_send.at[position],
            give_recv.at[position],
            sibling,
        )

    def compute_own(position):
        g_own[position] = compute(position, core)

    def compute_twin(position):
        for half in range(2):
            pair_copy(position, half, twin).wait_recv()
        g_give[position] = compute(position, twin).astype(BF16)
        give_copy(position).start()

    def both_ways(step, work):
        if step == 0:
            work(here)
            return

        @pl.loop(0, 2)
        def _(way):
            work(lax.rem(here + chips + (2 * way - 1) * step, chips))

    for step in range(1, far + 1):
        for half in range(2):
            for way in range(2):
                if travels(way, step, half):
                    ring_arrival(way, step, half).wait_recv()
                    if travels(way, step + 1, half):
                        send(ring_copy(way, step + 1, half))
                    send(pair_copy(at(-step if way == 0 else step), half, core))
            both_ways(step - 1, compute_own if half == 1 else compute_twin)

    def total_of(position, half):
        rows_of = pl.ds(half * piece, piece)
        return g_own[position, rows_of] + g_take[position, rows_of].astype(F32)

    def sum_copy(way, step, half):
        index = (way, step - 1, half)
        return remote(
            sum_out.at[index],
            sum_in.at[index],
            sum_send.at[index],
            sum_recv.at[index],
            after if way == 0 else before,
        )

    def send_sum(way, step, half):
        value = total_of(at(step if way == 0 else -step), half)
        if travels(way, step + 1, half):
            sum_copy(way, step + 1, half).wait_recv()
            value = value + sum_in[way, step, half].astype(F32)
        sum_out[way, step - 1, half] = value.astype(BF16)
        send(sum_copy(way, step, half))

    compute_twin(at(far))
    for step in (far - 1, 1 - far):
        give_copy(at(step)).wait_recv()
    for way in range(2):
        send_sum(way, far - 1, 1 - way)
    compute_own(at(far))

    for step in range(1, groups):
        target = lax.rem(series + step, groups)
        rows_of = pl.ds(pl.multiple_of(target * part, part), part)
        gx_out[step - 1] = gx[rows_of, :].astype(BF16)
        send(
            remote(
                gx_out.at[step - 1],
                gx_in.at[step - 1],
                gx_send.at[step - 1],
                gx_recv.at[step - 1],
                others[step - 1],
            )
        )

    give_copy(at(far)).wait_recv()
    for way in range(2):
        send_sum(way, far, way)

    span = width + REACH
    rim_copy.wait_recv()
    loads[3].wait()
    loads[4].wait()
    loads[8].wait()
    places = tm * width - REACH + lax.broadcasted_iota(jnp.int32, (K, span), 1)
    inside = places >= 0
    hidden = jnp.concatenate([rim[...].reshape(K, REACH), x_now], axis=1).astype(F32)
    hidden = jnp.where(inside, hidden, 0.0)

    def conv_layer(hidden, layer):
        hb = hidden.astype(BF16)
        past = pltpu.roll(hb.astype(F32), dil_ref[layer], 1).astype(BF16)
        z_val = jnp.dot(w_buf[layer, 0], past, preferred_element_type=F32)
        z_val = z_val + jnp.dot(w_buf[layer, 1], hb, preferred_element_type=F32)
        z_val = z_val + cb_buf[layer][:, None]
        return jnp.where(inside, hidden + jnp.maximum(z_val, 0.0), 0.0)

    layer = 0
    for step in range(far - 1, 0, -1):
        if layer < LAYERS:
            hidden = conv_layer(hidden, layer)
            layer += 1
        if step < far - 1:
            for offset in (step, -step):
                give_copy(at(offset)).wait_recv()
        for half in range(2):
            for way in range(2):
                if step < far - 1 or half == way:
                    send_sum(way, step, half)
    while layer < LAYERS:
        hidden = conv_layer(hidden, layer)
        layer += 1
    h_buf[...] = hidden[:, REACH:]

    own_rows = pl.ds(pl.multiple_of(series * part, part), part)
    grad_x = gx[own_rows, :]
    for step in range(1, groups):
        remote(
            gx_out.at[step - 1],
            gx_in.at[step - 1],
            gx_send.at[step - 1],
            gx_recv.at[step - 1],
            others[step - 1],
        ).wait_recv()
        grad_x = grad_x + gx_in[step - 1].astype(F32)
    grad_x = -grad_x * math.sqrt(K / total_series)
    basis = b_own[...]
    b_out[...] = basis - 0.5 * (grad_x + (basis - h_buf[own_rows, :]))
    stores = [
        pltpu.make_async_copy(source, target, load_sem.at[len(loads) + index])
        for index, (source, target) in enumerate(
            ((f_out, f_end), (m_out, m_end), (v_out, v_end), (b_out, b_end))
        )
    ]
    stores[3].start()

    loads[5].wait()
    loads[6].wait()
    give_copy(here).wait_recv()
    scale_f = 1.0 / math.sqrt(total_time)
    for half in range(2):
        rows_of = pl.ds(half * piece, piece)
        value = total_of(here, half)
        for way in range(2):
            sum_copy(way, 1, half).wait_recv()
            value = value + sum_in[way, 0, half].astype(F32)
        grad_f = -value * scale_f
        m_new = 0.9 * m_own[rows_of] + 0.1 * grad_f
        v_new = 0.999 * v_own[rows_of] + 0.001 * grad_f * grad_f
        m_hat = m_new / (1.0 - 0.9**10)
        v_hat = v_new / (1.0 - 0.999**10)
        f_out[rows_of] = f_own[rows_of] - 0.01 * m_hat / (jnp.sqrt(v_hat) + 1e-08)
        m_out[rows_of] = m_new
        v_out[rows_of] = v_new
    for store in stores[:3]:
        store.start()

    for copy in pending:
        copy.wait_send()

    @pl.loop(0, chips)
    def _(position):
        give_copy(position).wait_send()

    for store in stores:
        store.wait()


def hand_out(*refs):
    copies = [
        pltpu.make_async_copy(refs[index], refs[4 + index], refs[8].at[index]) for index in range(4)
    ]
    for copy in copies:
        copy.start()
    for copy in copies:
        copy.wait()


def on_device(count, groups, y_obs, tile_mask, factors, adam_m, adam_v, basis, dilations, conv_w, conv_b):
    rows = factors.shape[0]
    part, width = basis.shape
    chips = count // 2
    far = chips // 2
    piece = rows // 2
    dma = pltpu.SemaphoreType.DMA
    hbm = pl.BlockSpec(memory_space=pltpu.HBM)
    work = y_obs.shape[0] * width * K * 6
    results = pl.pallas_call(
        functools.partial(kernel, count, groups),
        out_shape=(
            jax.ShapeDtypeStruct(factors.shape, F32),
            jax.ShapeDtypeStruct(factors.shape, F32),
            jax.ShapeDtypeStruct(factors.shape, F32),
            jax.ShapeDtypeStruct(basis.shape, F32),
        ),
        in_specs=[hbm] * 9,
        out_specs=(hbm,) * 4,
        scratch_shapes=[
            pltpu.VMEM(factors.shape, F32),
            pltpu.VMEM(factors.shape, F32),
            pltpu.VMEM(factors.shape, F32),
            pltpu.VMEM(basis.shape, F32),
            pltpu.VMEM(y_obs.shape, BF16),
            pltpu.VMEM(tile_mask.shape[::-1], jnp.int32),
            pltpu.VMEM(tile_mask.shape, F32),
            pltpu.SMEM(dilations.shape, jnp.int32),
            pltpu.VMEM(factors.shape, F32),
            pltpu.VMEM(factors.shape, F32),
            pltpu.VMEM(factors.shape, F32),
            pltpu.VMEM(basis.shape, F32),
            pltpu.VMEM(conv_w.shape, BF16),
            pltpu.VMEM(conv_b.shape, F32),
            pltpu.VMEM((chips, 2, rows, K), BF16),
            pltpu.VMEM((groups, part, width), BF16),
            pltpu.VMEM((width, K), BF16),
            pltpu.VMEM((groups, part, REACH), BF16),
            pltpu.VMEM((chips, rows, K), F32),
            pltpu.VMEM((chips, rows, K), BF16),
            pltpu.VMEM((chips, rows, K), BF16),
            pltpu.VMEM((2, far, 2, piece, K), BF16),
            pltpu.VMEM((2, far, 2, piece, K), BF16),
            pltpu.VMEM((K, width), F32),
            pltpu.VMEM((max(groups - 1, 1), part, width), BF16),
            pltpu.VMEM((max(groups - 1, 1), part, width), BF16),
            pltpu.VMEM((K, width), F32),
            dma((13,)),
            dma((2, far, 2)),
            dma((2, far, 2)),
            dma((chips, 2)),
            dma((chips, 2)),
            dma((max(groups - 1, 1),)),
            dma((max(groups - 1, 1),)),
            dma((2,)),
            dma((chips,)),
            dma((chips,)),
            dma((2, far, 2)),
            dma((2, far, 2)),
            dma((max(groups - 1, 1),)),
            dma((max(groups - 1, 1),)),
        ],
        compiler_params=pltpu.CompilerParams(
            collective_id=0, has_side_effects=True, vmem_limit_bytes=60 * 2**20
        ),
        cost_estimate=pl.CostEstimate(
            flops=work, bytes_accessed=2 * y_obs.size, transcendentals=factors.size
        ),
    )(y_obs, tile_mask.T, factors, adam_m, adam_v, basis, dilations, conv_w, conv_b)
    return pl.pallas_call(
        hand_out,
        out_shape=tuple(jax.ShapeDtypeStruct(result.shape, F32) for result in results),
        in_specs=[hbm] * 4,
        out_specs=(hbm,) * 4,
        scratch_shapes=[dma((4,))],
        compiler_params=pltpu.CompilerParams(vmem_limit_bytes=60 * 2**20),
    )(*results)


def solution(mesh):
    return jax.shard_map(
        functools.partial(on_device, mesh.shape["tm"], mesh.shape["series"]),
        mesh=mesh,
        in_specs=(
            P("series", "tm"),
            P("series", "tm"),
            P(("series", "tm"), None),
            P(("series", "tm"), None),
            P(("series", "tm"), None),
            P("series", "tm"),
            P(),
            P(),
            P(),
        ),
        out_specs=(
            P(("series", "tm"), None),
            P(("series", "tm"), None),
            P(("series", "tm"), None),
            P("series", "tm"),
        ),
        check_vma=False,
    )
```

```python
import functools
import math

import jax
import jax.numpy as jnp
from jax import lax
from jax.experimental import pallas as pl
from jax.experimental.pallas import tpu as pltpu
from jax.sharding import PartitionSpec as P

K = 128
TILE = 128
LAYERS = 4
D_MAX = 32
REACH = LAYERS * D_MAX
MESH = pl.DeviceIdType.MESH
F32 = jnp.float32
BF16 = jnp.bfloat16


def kernel(
    count,
    groups,
    y_hbm,
    mask_hbm,
    f_hbm,
    m_hbm,
    v_hbm,
    b_hbm,
    dil_hbm,
    w_hbm,
    cb_hbm,
    f_end,
    m_end,
    v_end,
    b_end,
    f_out,
    m_out,
    v_out,
    b_out,
    y_buf,
    mask_in,
    mask_ref,
    dil_ref,
    f_own,
    m_own,
    v_own,
    b_own,
    w_buf,
    cb_buf,
    f_buf,
    x_buf,
    xt_buf,
    rim,
    g_own,
    g_give,
    g_take,
    y_sum_out,
    y_sum_in,
    z_sum_out,
    z_sum_in,
    gx,
    gx_out,
    gx_in,
    h_buf,
    load_sem,
    z_send,
    z_recv,
    y_send,
    y_recv,
    pair_send,
    pair_recv,
    x_send,
    x_recv,
    rim_sem,
    give_send,
    give_recv,
    y_sum_send,
    y_sum_recv,
    z_sum_send,
    z_sum_recv,
    gx_send,
    gx_recv,
):
    side = count // 4
    rows = f_own.shape[0]
    part, width = b_own.shape
    total_time = width * count
    total_series = rows * count * groups

    series = lax.axis_index("series")
    tm = lax.axis_index("tm")
    core = lax.rem(tm, 2)
    twin = 1 - core
    y_at = lax.rem(tm // 2, 2)
    over = 1 - y_at
    z_at = tm // 4

    def column(step):
        return lax.rem(z_at + side + step, side)

    def member(z, y, which):
        return (series, 4 * z + 2 * y + which)

    sibling = member(z_at, y_at, twin)
    across = member(z_at, over, core)
    ahead = [member(column(step), y_at, core) for step in range(side)]
    behind = [member(column(-step), y_at, core) for step in range(side)]
    following = (series, lax.rem(tm + 1, count))
    preceding = (series, lax.rem(tm + count - 1, count))

    loads = [
        pltpu.make_async_copy(source, target, load_sem.at[index])
        for index, (source, target) in enumerate(
            (
                (b_hbm, b_own),
                (f_hbm, f_own),
                (y_hbm, y_buf),
                (w_hbm, w_buf),
                (cb_hbm, cb_buf),
                (m_hbm, m_own),
                (v_hbm, v_own),
                (mask_hbm, mask_in),
                (dil_hbm, dil_ref),
            )
        )
    ]
    for load in loads:
        load.start()

    barrier = pltpu.get_barrier_semaphore()
    others = [(lax.rem(series + step, groups), tm) for step in range(1, groups)]
    greeted = ahead[1:] + [across, sibling, following, preceding] + others
    for device in greeted:
        pl.semaphore_signal(barrier, inc=1, device_id=device, device_id_type=MESH)
    loads[1].wait()
    f_buf[z_at, y_at, core] = f_own[...].astype(BF16)
    loads[0].wait()
    x_buf[series] = b_own[...].astype(BF16)
    gx[...] = jnp.zeros_like(gx)
    pl.semaphore_wait(barrier, len(greeted))

    def remote(source, target, send, recv, device):
        return pltpu.make_async_remote_copy(
            src_ref=source,
            dst_ref=target,
            send_sem=send,
            recv_sem=recv,
            device_id=device,
            device_id_type=MESH,
        )

    pending = []

    def send(copy):
        copy.start()
        pending.append(copy)

    def same(ref, sends, recvs, index, device):
        return remote(ref, ref, sends.at[index], recvs.at[index], device)

    def z_arrival(step):
        ref = f_buf.at[column(-step), y_at, core]
        same(ref, z_send, z_recv, step - 1, ahead[step]).wait_recv()
        pass_on(step)

    def pass_on(step):
        ref = f_buf.at[column(-step), y_at, core]
        send(same(ref, y_send, y_recv, step, across))
        send(same(ref, pair_send, pair_recv, (step, 0), sibling))

    def y_arrival(step):
        ref = f_buf.at[column(-step), over, core]
        same(ref, y_send, y_recv, step, across).wait_recv()
        send(same(ref, pair_send, pair_recv, (step, 1), sibling))

    for step in range(1, side):
        ref = f_buf.at[z_at, y_at, core]
        send(same(ref, z_send, z_recv, step - 1, ahead[step]))
        if step == 1:
            pass_on(0)
    for step in range(1, groups):
        send(
            remote(
                x_buf.at[series],
                x_buf.at[series],
                x_send.at[step - 1],
                x_recv.at[step - 1],
                others[step - 1],
            )
        )
    for step in range(1, groups):
        origin = lax.rem(series + groups - step, groups)
        remote(
            x_buf.at[origin],
            x_buf.at[origin],
            x_send.at[step - 1],
            x_recv.at[step - 1],
            others[step - 1],
        ).wait_recv()
    rim_copy = remote(
        x_buf.at[:, :, pl.ds(width - REACH, REACH)],
        rim,
        rim_sem.at[0],
        rim_sem.at[1],
        following,
    )

    @pl.when(tm < count - 1)
    def _():
        rim_copy.start()

    x_now = x_buf[...].reshape(K, width)
    xt_buf[...] = x_now.astype(F32).T.astype(BF16)
    loads[2].wait()
    loads[7].wait()
    mask_ref[...] = mask_in[...].astype(F32).T

    band = min(rows, TILE)

    def compute(z, y, which):
        block = 4 * z + 2 * y + which
        f_now = f_buf[z, y, which]
        x_full = x_buf[...].reshape(K, width)
        pred = jnp.dot(f_now, x_full, preferred_element_type=F32)
        parts = []
        for index in range(rows // band):
            start = pl.multiple_of(block * rows + index * band, band)
            tile_row = start // TILE
            y_now = y_buf[pl.ds(start, band), :].astype(F32)
            flags = mask_ref[pl.ds(tile_row, 1), :]
            seen = jnp.concatenate(
                [
                    jnp.broadcast_to(flags[:, column : column + 1], (1, TILE))
                    for column in range(width // TILE)
                ],
                axis=1,
            )
            inner = pred[index * band : (index + 1) * band]
            parts.append((seen * (y_now - inner)).astype(BF16))
        rb = jnp.concatenate(parts, axis=0) if len(parts) > 1 else parts[0]
        gx[...] += lax.dot_general(
            f_now, rb, (((0,), (0,)), ((), ())), preferred_element_type=F32
        )
        return jnp.dot(rb, xt_buf[...], preferred_element_type=F32)

    def own_block(step, row):
        g_own[step, row] = compute(column(-step), over if row else y_at, core)

    def give_copy(step, row):
        index = (step, row)
        return remote(
            g_give.at[index], g_take.at[index], give_send.at[index], give_recv.at[index], sibling
        )

    def twin_block(step, row):
        z, y = column(-step), over if row else y_at
        same(f_buf.at[z, y, twin], pair_send, pair_recv, (step, row), sibling).wait_recv()
        g_give[step, row] = compute(z, y, twin).astype(BF16)
        send(give_copy(step, row))

    def pair_total(step, row):
        give_copy(step, row).wait_recv()
        return g_own[step, row] + g_take[step, row].astype(F32)

    def y_sum_copy(step):
        return remote(
            y_sum_out.at[step],
            y_sum_in.at[step],
            y_sum_send.at[step],
            y_sum_recv.at[step],
            across,
        )

    def y_send_sum(step):
        y_sum_out[step] = pair_total(step, 1).astype(BF16)
        send(y_sum_copy(step))

    def chip_total(step):
        total = pair_total(step, 0)
        y_sum_copy(step).wait_recv()
        return total + y_sum_in[step].astype(F32)

    def z_sum_copy(step):
        return remote(
            z_sum_out.at[step - 1],
            z_sum_in.at[step - 1],
            z_sum_send.at[step - 1],
            z_sum_recv.at[step - 1],
            behind[step],
        )

    def z_send_sum(step):
        z_sum_out[step - 1] = chip_total(step).astype(BF16)
        send(z_sum_copy(step))

    own_block(0, 0)
    z_arrival(1)
    y_arrival(0)
    twin_block(0, 0)
    if side > 2:
        z_arrival(2)
    own_block(0, 1)
    if side > 3:
        z_arrival(3)
    y_arrival(1)
    twin_block(0, 1)
    for step in range(1, side):
        if step + 3 < side:
            z_arrival(step + 3)
        if step + 1 < side:
            y_arrival(step + 1)
        twin_block(step, 1)
        if step == 1:
            y_send_sum(0)
        own_block(step, 1)
        if step > 1:
            z_send_sum(step - 1)
        twin_block(step, 0)
        y_send_sum(step)
        own_block(step, 0)

    for step in range(1, groups):
        target = lax.rem(series + step, groups)
        rows_of = pl.ds(pl.multiple_of(target * part, part), part)
        gx_out[step - 1] = gx[rows_of, :].astype(BF16)
        send(
            remote(
                gx_out.at[step - 1],
                gx_in.at[step - 1],
                gx_send.at[step - 1],
                gx_recv.at[step - 1],
                others[step - 1],
            )
        )

    span = width + REACH
    @pl.when(tm > 0)
    def _():
        rim_copy.wait_recv()

    loads[3].wait()
    loads[4].wait()
    loads[8].wait()
    places = tm * width - REACH + lax.broadcasted_iota(jnp.int32, (K, span), 1)
    inside = places >= 0
    hidden = jnp.concatenate([rim[...].reshape(K, REACH), x_now], axis=1).astype(F32)
    hidden = jnp.where(inside, hidden, 0.0)

    def conv_layer(hidden, layer):
        hb = hidden.astype(BF16)
        past = pltpu.roll(hb.astype(F32), dil_ref[layer], 1).astype(BF16)
        z_val = jnp.dot(w_buf[layer, 0], past, preferred_element_type=F32)
        z_val = z_val + jnp.dot(w_buf[layer, 1], hb, preferred_element_type=F32)
        z_val = z_val + cb_buf[layer][:, None]
        return jnp.where(inside, hidden + jnp.maximum(z_val, 0.0), 0.0)

    for layer in range(LAYERS):
        if layer == LAYERS // 2:
            z_send_sum(side - 1)
        hidden = conv_layer(hidden, layer)
    h_buf[...] = hidden[:, REACH:]

    own_rows = pl.ds(pl.multiple_of(series * part, part), part)
    grad_x = gx[own_rows, :]
    for step in range(1, groups):
        remote(
            gx_out.at[step - 1],
            gx_in.at[step - 1],
            gx_send.at[step - 1],
            gx_recv.at[step - 1],
            others[step - 1],
        ).wait_recv()
        grad_x = grad_x + gx_in[step - 1].astype(F32)
    grad_x = -grad_x * math.sqrt(K / total_series)
    basis = b_own[...]
    b_out[...] = basis - 0.5 * (grad_x + (basis - h_buf[own_rows, :]))
    stores = [
        pltpu.make_async_copy(source, target, load_sem.at[len(loads) + index])
        for index, (source, target) in enumerate(
            ((f_out, f_end), (m_out, m_end), (v_out, v_end), (b_out, b_end))
        )
    ]
    stores[3].start()

    loads[5].wait()
    loads[6].wait()
    scale_f = 1.0 / math.sqrt(total_time)
    value = chip_total(0)
    for step in range(1, side):
        z_sum_copy(step).wait_recv()
        value = value + z_sum_in[step - 1].astype(F32)
    grad_f = -value * scale_f
    m_new = 0.9 * m_own[...] + 0.1 * grad_f
    v_new = 0.999 * v_own[...] + 0.001 * grad_f * grad_f
    m_hat = m_new / (1.0 - 0.9**10)
    v_hat = v_new / (1.0 - 0.999**10)
    f_out[...] = f_own[...] - 0.01 * m_hat / (jnp.sqrt(v_hat) + 1e-08)
    m_out[...] = m_new
    v_out[...] = v_new
    for store in stores[:3]:
        store.start()

    for copy in pending:
        copy.wait_send()

    @pl.when(tm < count - 1)
    def _():
        rim_copy.wait_send()

    for store in stores:
        store.wait()


def hand_out(*refs):
    sources, targets, held, sem = refs[:4], refs[4:8], refs[8:12], refs[12]
    loads = [pltpu.make_async_copy(sources[i], held[i], sem.at[i]) for i in range(4)]
    stores = [pltpu.make_async_copy(held[i], targets[i], sem.at[4 + i]) for i in range(4)]
    for load in loads:
        load.start()
    for load, store in zip(loads, stores):
        load.wait()
        store.start()
    for store in stores:
        store.wait()


def on_device(count, groups, y_obs, tile_mask, factors, adam_m, adam_v, basis, dilations, conv_w, conv_b):
    rows = factors.shape[0]
    part, width = basis.shape
    side = count // 4
    dma = pltpu.SemaphoreType.DMA
    hbm = pl.BlockSpec(memory_space=pltpu.HBM)
    work = y_obs.shape[0] * width * K * 6
    results = pl.pallas_call(
        functools.partial(kernel, count, groups),
        out_shape=(
            jax.ShapeDtypeStruct(factors.shape, F32),
            jax.ShapeDtypeStruct(factors.shape, F32),
            jax.ShapeDtypeStruct(factors.shape, F32),
            jax.ShapeDtypeStruct(basis.shape, F32),
        ),
        in_specs=[hbm] * 9,
        out_specs=(hbm,) * 4,
        scratch_shapes=[
            pltpu.VMEM(factors.shape, F32),
            pltpu.VMEM(factors.shape, F32),
            pltpu.VMEM(factors.shape, F32),
            pltpu.VMEM(basis.shape, F32),
            pltpu.VMEM(y_obs.shape, BF16),
            pltpu.VMEM(tile_mask.shape[::-1], jnp.int32),
            pltpu.VMEM(tile_mask.shape, F32),
            pltpu.SMEM(dilations.shape, jnp.int32),
            pltpu.VMEM(factors.shape, F32),
            pltpu.VMEM(factors.shape, F32),
            pltpu.VMEM(factors.shape, F32),
            pltpu.VMEM(basis.shape, F32),
            pltpu.VMEM(conv_w.shape, BF16),
            pltpu.VMEM(conv_b.shape, F32),
            pltpu.VMEM((side, 2, 2, rows, K), BF16),
            pltpu.VMEM((groups, part, width), BF16),
            pltpu.VMEM((width, K), BF16),
            pltpu.VMEM((groups, part, REACH), BF16),
            pltpu.VMEM((side, 2, rows, K), F32),
            pltpu.VMEM((side, 2, rows, K), BF16),
            pltpu.VMEM((side, 2, rows, K), BF16),
            pltpu.VMEM((side, rows, K), BF16),
            pltpu.VMEM((side, rows, K), BF16),
            pltpu.VMEM((side - 1, rows, K), BF16),
            pltpu.VMEM((side - 1, rows, K), BF16),
            pltpu.VMEM((K, width), F32),
            pltpu.VMEM((max(groups - 1, 1), part, width), BF16),
            pltpu.VMEM((max(groups - 1, 1), part, width), BF16),
            pltpu.VMEM((K, width), F32),
            dma((13,)),
            dma((side - 1,)),
            dma((side - 1,)),
            dma((side,)),
            dma((side,)),
            dma((side, 2)),
            dma((side, 2)),
            dma((max(groups - 1, 1),)),
            dma((max(groups - 1, 1),)),
            dma((2,)),
            dma((side, 2)),
            dma((side, 2)),
            dma((side,)),
            dma((side,)),
            dma((side - 1,)),
            dma((side - 1,)),
            dma((max(groups - 1, 1),)),
            dma((max(groups - 1, 1),)),
        ],
        compiler_params=pltpu.CompilerParams(
            collective_id=0, has_side_effects=True, vmem_limit_bytes=60 * 2**20
        ),
        cost_estimate=pl.CostEstimate(
            flops=work, bytes_accessed=2 * y_obs.size, transcendentals=factors.size
        ),
    )(y_obs, tile_mask.T, factors, adam_m, adam_v, basis, dilations, conv_w, conv_b)
    return pl.pallas_call(
        hand_out,
        out_shape=tuple(jax.ShapeDtypeStruct(result.shape, F32) for result in results),
        in_specs=[hbm] * 4,
        out_specs=(hbm,) * 4,
        scratch_shapes=[pltpu.VMEM(result.shape, F32) for result in results] + [dma((8,))],
        compiler_params=pltpu.CompilerParams(vmem_limit_bytes=60 * 2**20),
    )(*results)


def solution(mesh):
    return jax.shard_map(
        functools.partial(on_device, mesh.shape["tm"], mesh.shape["series"]),
        mesh=mesh,
        in_specs=(
            P("series", "tm"),
            P("series", "tm"),
            P(("series", "tm"), None),
            P(("series", "tm"), None),
            P(("series", "tm"), None),
            P("series", "tm"),
            P(),
            P(),
            P(),
        ),
        out_specs=(
            P(("series", "tm"), None),
            P(("series", "tm"), None),
            P(("series", "tm"), None),
            P("series", "tm"),
        ),
        check_vma=False,
    )
```

```python
import functools
import math

import jax
import jax.numpy as jnp
from jax import lax
from jax.experimental import pallas as pl
from jax.experimental.pallas import tpu as pltpu
from jax.sharding import PartitionSpec as P

K = 128
TILE = 128
LAYERS = 4
D_MAX = 32
REACH = LAYERS * D_MAX
MESH = pl.DeviceIdType.MESH
F32 = jnp.float32
BF16 = jnp.bfloat16


def kernel(
    count,
    groups,
    y_hbm,
    mask_hbm,
    f_hbm,
    m_hbm,
    v_hbm,
    b_hbm,
    dil_hbm,
    w_hbm,
    cb_hbm,
    f_end,
    m_end,
    v_end,
    b_end,
    f_out,
    m_out,
    v_out,
    b_out,
    y_buf,
    mask_in,
    mask_ref,
    dil_ref,
    f_own,
    m_own,
    v_own,
    b_own,
    w_buf,
    cb_buf,
    f_buf,
    x_buf,
    xt_buf,
    rim,
    g_both,
    g_own,
    g_give,
    g_take,
    y_sum_out,
    y_sum_in,
    z_sum_out,
    z_sum_in,
    gx,
    gx_out,
    gx_in,
    h_buf,
    load_sem,
    z_send,
    z_recv,
    y_send,
    y_recv,
    pair_send,
    pair_recv,
    x_send,
    x_recv,
    rim_sem,
    give_send,
    give_recv,
    y_sum_send,
    y_sum_recv,
    z_sum_send,
    z_sum_recv,
    gx_send,
    gx_recv,
):
    side = count // 4
    rows = f_own.shape[0]
    part, width = b_own.shape
    total_time = width * count
    total_series = rows * count * groups

    series = lax.axis_index("series")
    tm = lax.axis_index("tm")
    core = lax.rem(tm, 2)
    twin = 1 - core
    y_at = lax.rem(tm // 2, 2)
    over = 1 - y_at
    z_at = tm // 4

    def column(step):
        return lax.rem(z_at + side + step, side)

    def member(z, y, which):
        return (series, 4 * z + 2 * y + which)

    sibling = member(z_at, y_at, twin)
    across = member(z_at, over, core)
    ahead = [member(column(step), y_at, core) for step in range(side)]
    behind = [member(column(-step), y_at, core) for step in range(side)]
    following = (series, lax.rem(tm + 1, count))
    preceding = (series, lax.rem(tm + count - 1, count))

    loads = [
        pltpu.make_async_copy(source, target, load_sem.at[index])
        for index, (source, target) in enumerate(
            (
                (b_hbm, b_own),
                (f_hbm, f_own),
                (y_hbm, y_buf),
                (w_hbm, w_buf),
                (cb_hbm, cb_buf),
                (m_hbm, m_own),
                (v_hbm, v_own),
                (mask_hbm, mask_in),
                (dil_hbm, dil_ref),
            )
        )
    ]
    for load in loads:
        load.start()

    barrier = pltpu.get_barrier_semaphore()
    others = [(lax.rem(series + step, groups), tm) for step in range(1, groups)]
    greeted = ahead[1:] + [across, sibling] + others
    for device in greeted:
        pl.semaphore_signal(barrier, inc=1, device_id=device, device_id_type=MESH)

    @pl.when(tm > 0)
    def _():
        pl.semaphore_signal(barrier, inc=1, device_id=preceding, device_id_type=MESH)

    loads[1].wait()
    f_buf[z_at, y_at, core] = f_own[...].astype(BF16)
    loads[0].wait()
    x_buf[series] = b_own[...].astype(BF16)
    gx[...] = jnp.zeros_like(gx)
    pl.semaphore_wait(barrier, len(greeted) + jnp.where(tm < count - 1, 1, 0))

    def remote(source, target, send, recv, device):
        return pltpu.make_async_remote_copy(
            src_ref=source,
            dst_ref=target,
            send_sem=send,
            recv_sem=recv,
            device_id=device,
            device_id_type=MESH,
        )

    pending = []

    def send(copy):
        copy.start()
        pending.append(copy)

    def same(ref, sends, recvs, index, device):
        return remote(ref, ref, sends.at[index], recvs.at[index], device)

    def z_arrival(step):
        ref = f_buf.at[column(-step), y_at, core]
        same(ref, z_send, z_recv, step - 1, ahead[step]).wait_recv()
        pass_on(step)

    def pass_on(step):
        ref = f_buf.at[column(-step), y_at, core]
        send(same(ref, y_send, y_recv, step, across))
        send(same(ref, pair_send, pair_recv, (step, 0), sibling))

    def y_arrival(step):
        ref = f_buf.at[column(-step), over, core]
        same(ref, y_send, y_recv, step, across).wait_recv()
        send(same(ref, pair_send, pair_recv, (step, 1), sibling))

    for step in range(1, groups):
        send(
            remote(
                x_buf.at[series],
                x_buf.at[series],
                x_send.at[step - 1],
                x_recv.at[step - 1],
                others[step - 1],
            )
        )
    for step in range(1, side):
        ref = f_buf.at[z_at, y_at, core]
        send(same(ref, z_send, z_recv, step - 1, ahead[step]))
        if step == 1:
            pass_on(0)

    for step in range(1, groups):
        origin = lax.rem(series + groups - step, groups)
        remote(
            x_buf.at[origin],
            x_buf.at[origin],
            x_send.at[step - 1],
            x_recv.at[step - 1],
            others[step - 1],
        ).wait_recv()
    rim_copy = remote(
        x_buf.at[:, :, pl.ds(width - REACH, REACH)],
        rim,
        rim_sem.at[0],
        rim_sem.at[1],
        following,
    )

    @pl.when(tm < count - 1)
    def _():
        rim_copy.start()

    x_now = x_buf[...].reshape(K, width)
    xt_buf[...] = x_now.astype(F32).T.astype(BF16)
    loads[2].wait()
    loads[7].wait()
    mask_ref[...] = mask_in[...].astype(F32).T

    band = min(2 * rows, 2 * TILE)

    def compute(z, y):
        first = (4 * z + 2 * y) * rows
        f_now = f_buf[z, y].reshape(2 * rows, K)
        x_full = x_buf[...].reshape(K, width)
        parts = []
        for start in range(0, 2 * rows, band):
            pred = jnp.dot(f_now[start : start + band], x_full, preferred_element_type=F32)
            for inner in range(0, band, TILE):
                at = pl.multiple_of(first + start + inner, TILE)
                y_now = y_buf[pl.ds(at, TILE), :].astype(F32)
                flags = mask_ref[pl.ds(at // TILE, 1), :]
                seen = jnp.concatenate(
                    [
                        jnp.broadcast_to(flags[:, column : column + 1], (1, TILE))
                        for column in range(width // TILE)
                    ],
                    axis=1,
                )
                parts.append((seen * (y_now - pred[inner : inner + TILE])).astype(BF16))
        rb = jnp.concatenate(parts, axis=0) if len(parts) > 1 else parts[0]
        gx[...] += lax.dot_general(
            f_now, rb, (((0,), (0,)), ((), ())), preferred_element_type=F32
        )
        return jnp.dot(rb, xt_buf[...], preferred_element_type=F32)

    def give_copy(step, row):
        index = (step, row)
        return remote(
            g_give.at[index], g_take.at[index], give_send.at[index], give_recv.at[index], sibling
        )

    def block(step, row):
        z, y = column(-step), over if row else y_at
        same(f_buf.at[z, y, twin], pair_send, pair_recv, (step, row), sibling).wait_recv()
        g_both[...] = compute(z, y).reshape(2, rows, K)
        g_give[step, row] = g_both[twin].astype(BF16)
        send(give_copy(step, row))
        g_own[step, row] = g_both[core]

    def pair_total(step, row):
        give_copy(step, row).wait_recv()
        return g_own[step, row] + g_take[step, row].astype(F32)

    def y_sum_copy(step):
        return remote(
            y_sum_out.at[step],
            y_sum_in.at[step],
            y_sum_send.at[step],
            y_sum_recv.at[step],
            across,
        )

    def y_send_sum(step):
        y_sum_out[step] = pair_total(step, 1).astype(BF16)
        send(y_sum_copy(step))

    def chip_total(step):
        total = pair_total(step, 0)
        y_sum_copy(step).wait_recv()
        return total + y_sum_in[step].astype(F32)

    def z_sum_copy(step):
        return remote(
            z_sum_out.at[step - 1],
            z_sum_in.at[step - 1],
            z_sum_send.at[step - 1],
            z_sum_recv.at[step - 1],
            behind[step],
        )

    def z_send_sum(step):
        z_sum_out[step - 1] = chip_total(step).astype(BF16)
        send(z_sum_copy(step))

    block(0, 0)
    z_arrival(1)
    y_arrival(0)
    if side > 2:
        z_arrival(2)
    block(0, 1)
    if side > 3:
        z_arrival(3)
    y_arrival(1)
    for step in range(1, side):
        if step + 3 < side:
            z_arrival(step + 3)
        if step + 1 < side:
            y_arrival(step + 1)
        block(step, 1)
        if step == 1:
            y_send_sum(0)
        else:
            z_send_sum(step - 1)
        block(step, 0)
        y_send_sum(step)

    for step in range(1, groups):
        target = lax.rem(series + step, groups)
        rows_of = pl.ds(pl.multiple_of(target * part, part), part)
        gx_out[step - 1] = gx[rows_of, :].astype(BF16)
        send(
            remote(
                gx_out.at[step - 1],
                gx_in.at[step - 1],
                gx_send.at[step - 1],
                gx_recv.at[step - 1],
                others[step - 1],
            )
        )

    span = width + REACH
    @pl.when(tm > 0)
    def _():
        rim_copy.wait_recv()

    loads[3].wait()
    loads[4].wait()
    loads[8].wait()
    places = tm * width - REACH + lax.broadcasted_iota(jnp.int32, (K, span), 1)
    inside = places >= 0
    hidden = jnp.concatenate([rim[...].reshape(K, REACH), x_now], axis=1).astype(F32)
    hidden = jnp.where(inside, hidden, 0.0)

    def conv_layer(hidden, layer):
        hb = hidden.astype(BF16)
        past = pltpu.roll(hb.astype(F32), dil_ref[layer], 1).astype(BF16)
        z_val = jnp.dot(w_buf[layer, 0], past, preferred_element_type=F32)
        z_val = z_val + jnp.dot(w_buf[layer, 1], hb, preferred_element_type=F32)
        z_val = z_val + cb_buf[layer][:, None]
        return jnp.where(inside, hidden + jnp.maximum(z_val, 0.0), 0.0)

    for layer in range(LAYERS):
        if layer == LAYERS // 2:
            z_send_sum(side - 1)
        hidden = conv_layer(hidden, layer)
    h_buf[...] = hidden[:, REACH:]

    own_rows = pl.ds(pl.multiple_of(series * part, part), part)
    grad_x = gx[own_rows, :]
    for step in range(1, groups):
        remote(
            gx_out.at[step - 1],
            gx_in.at[step - 1],
            gx_send.at[step - 1],
            gx_recv.at[step - 1],
            others[step - 1],
        ).wait_recv()
        grad_x = grad_x + gx_in[step - 1].astype(F32)
    grad_x = -grad_x * math.sqrt(K / total_series)
    basis = b_own[...]
    b_out[...] = basis - 0.5 * (grad_x + (basis - h_buf[own_rows, :]))
    stores = [
        pltpu.make_async_copy(source, target, load_sem.at[len(loads) + index])
        for index, (source, target) in enumerate(
            ((f_out, f_end), (m_out, m_end), (v_out, v_end), (b_out, b_end))
        )
    ]
    stores[3].start()

    loads[5].wait()
    loads[6].wait()
    scale_f = 1.0 / math.sqrt(total_time)
    value = chip_total(0)
    for step in range(1, side):
        z_sum_copy(step).wait_recv()
        value = value + z_sum_in[step - 1].astype(F32)
    grad_f = -value * scale_f
    m_new = 0.9 * m_own[...] + 0.1 * grad_f
    v_new = 0.999 * v_own[...] + 0.001 * grad_f * grad_f
    m_hat = m_new / (1.0 - 0.9**10)
    v_hat = v_new / (1.0 - 0.999**10)
    f_out[...] = f_own[...] - 0.01 * m_hat / (jnp.sqrt(v_hat) + 1e-08)
    m_out[...] = m_new
    v_out[...] = v_new
    for store in stores[:3]:
        store.start()

    for copy in pending:
        copy.wait_send()

    @pl.when(tm < count - 1)
    def _():
        rim_copy.wait_send()

    for store in stores:
        store.wait()


def hand_out(*refs):
    sources, targets, held, sem = refs[:4], refs[4:8], refs[8:12], refs[12]
    loads = [pltpu.make_async_copy(sources[i], held[i], sem.at[i]) for i in range(4)]
    stores = [pltpu.make_async_copy(held[i], targets[i], sem.at[4 + i]) for i in range(4)]
    for load in loads:
        load.start()
    for load, store in zip(loads, stores):
        load.wait()
        store.start()
    for store in stores:
        store.wait()


def on_device(count, groups, y_obs, tile_mask, factors, adam_m, adam_v, basis, dilations, conv_w, conv_b):
    rows = factors.shape[0]
    part, width = basis.shape
    side = count // 4
    dma = pltpu.SemaphoreType.DMA
    hbm = pl.BlockSpec(memory_space=pltpu.HBM)
    work = y_obs.shape[0] * width * K * 6
    results = pl.pallas_call(
        functools.partial(kernel, count, groups),
        out_shape=(
            jax.ShapeDtypeStruct(factors.shape, F32),
            jax.ShapeDtypeStruct(factors.shape, F32),
            jax.ShapeDtypeStruct(factors.shape, F32),
            jax.ShapeDtypeStruct(basis.shape, F32),
        ),
        in_specs=[hbm] * 9,
        out_specs=(hbm,) * 4,
        scratch_shapes=[
            pltpu.VMEM(factors.shape, F32),
            pltpu.VMEM(factors.shape, F32),
            pltpu.VMEM(factors.shape, F32),
            pltpu.VMEM(basis.shape, F32),
            pltpu.VMEM(y_obs.shape, BF16),
            pltpu.VMEM(tile_mask.shape[::-1], jnp.int32),
            pltpu.VMEM(tile_mask.shape, F32),
            pltpu.SMEM(dilations.shape, jnp.int32),
            pltpu.VMEM(factors.shape, F32),
            pltpu.VMEM(factors.shape, F32),
            pltpu.VMEM(factors.shape, F32),
            pltpu.VMEM(basis.shape, F32),
            pltpu.VMEM(conv_w.shape, BF16),
            pltpu.VMEM(conv_b.shape, F32),
            pltpu.VMEM((side, 2, 2, rows, K), BF16),
            pltpu.VMEM((groups, part, width), BF16),
            pltpu.VMEM((width, K), BF16),
            pltpu.VMEM((groups, part, REACH), BF16),
            pltpu.VMEM((2, rows, K), F32),
            pltpu.VMEM((side, 2, rows, K), F32),
            pltpu.VMEM((side, 2, rows, K), BF16),
            pltpu.VMEM((side, 2, rows, K), BF16),
            pltpu.VMEM((side, rows, K), BF16),
            pltpu.VMEM((side, rows, K), BF16),
            pltpu.VMEM((side - 1, rows, K), BF16),
            pltpu.VMEM((side - 1, rows, K), BF16),
            pltpu.VMEM((K, width), F32),
            pltpu.VMEM((max(groups - 1, 1), part, width), BF16),
            pltpu.VMEM((max(groups - 1, 1), part, width), BF16),
            pltpu.VMEM((K, width), F32),
            dma((13,)),
            dma((side - 1,)),
            dma((side - 1,)),
            dma((side,)),
            dma((side,)),
            dma((side, 2)),
            dma((side, 2)),
            dma((max(groups - 1, 1),)),
            dma((max(groups - 1, 1),)),
            dma((2,)),
            dma((side, 2)),
            dma((side, 2)),
            dma((side,)),
            dma((side,)),
            dma((side - 1,)),
            dma((side - 1,)),
            dma((max(groups - 1, 1),)),
            dma((max(groups - 1, 1),)),
        ],
        compiler_params=pltpu.CompilerParams(
            collective_id=0, has_side_effects=True, vmem_limit_bytes=60 * 2**20
        ),
        cost_estimate=pl.CostEstimate(
            flops=work, bytes_accessed=2 * y_obs.size, transcendentals=factors.size
        ),
    )(y_obs, tile_mask.T, factors, adam_m, adam_v, basis, dilations, conv_w, conv_b)
    return pl.pallas_call(
        hand_out,
        out_shape=tuple(jax.ShapeDtypeStruct(result.shape, F32) for result in results),
        in_specs=[hbm] * 4,
        out_specs=(hbm,) * 4,
        scratch_shapes=[pltpu.VMEM(result.shape, F32) for result in results] + [dma((8,))],
        compiler_params=pltpu.CompilerParams(vmem_limit_bytes=60 * 2**20),
    )(*results)


def solution(mesh):
    return jax.shard_map(
        functools.partial(on_device, mesh.shape["tm"], mesh.shape["series"]),
        mesh=mesh,
        in_specs=(
            P("series", "tm"),
            P("series", "tm"),
            P(("series", "tm"), None),
            P(("series", "tm"), None),
            P(("series", "tm"), None),
            P("series", "tm"),
            P(),
            P(),
            P(),
        ),
        out_specs=(
            P(("series", "tm"), None),
            P(("series", "tm"), None),
            P(("series", "tm"), None),
            P("series", "tm"),
        ),
        check_vma=False,
    )
```

```python
import functools
import math

import jax
import jax.numpy as jnp
from jax import lax
from jax.experimental import pallas as pl
from jax.experimental.pallas import tpu as pltpu
from jax.sharding import PartitionSpec as P

K = 128
TILE = 128
LAYERS = 4
D_MAX = 32
REACH = LAYERS * D_MAX
MESH = pl.DeviceIdType.MESH
F32 = jnp.float32
BF16 = jnp.bfloat16


def kernel(
    count,
    groups,
    y_hbm,
    mask_hbm,
    f_hbm,
    m_hbm,
    v_hbm,
    b_hbm,
    dil_hbm,
    w_hbm,
    cb_hbm,
    f_end,
    m_end,
    v_end,
    b_end,
    f_out,
    m_out,
    v_out,
    b_out,
    y_buf,
    mask_in,
    mask_ref,
    dil_ref,
    f_own,
    m_own,
    v_own,
    b_own,
    w_buf,
    cb_buf,
    f_buf,
    x_buf,
    xt_buf,
    rim,
    g_both,
    g_own,
    g_give,
    g_take,
    y_sum_out,
    y_sum_in,
    z_sum_out,
    z_sum_in,
    gx,
    gx_out,
    gx_in,
    h_buf,
    load_sem,
    z_send,
    z_recv,
    y_send,
    y_recv,
    pair_send,
    pair_recv,
    x_send,
    x_recv,
    rim_sem,
    give_send,
    give_recv,
    y_sum_send,
    y_sum_recv,
    z_sum_send,
    z_sum_recv,
    gx_send,
    gx_recv,
):
    side = count // 4
    rows = f_own.shape[0]
    part, width = b_own.shape
    total_time = width * count
    total_series = rows * count * groups

    series = lax.axis_index("series")
    tm = lax.axis_index("tm")
    core = lax.rem(tm, 2)
    twin = 1 - core
    y_at = lax.rem(tm // 2, 2)
    over = 1 - y_at
    z_at = tm // 4

    def column(step):
        return lax.rem(z_at + side + step, side)

    def member(z, y, which):
        return (series, 4 * z + 2 * y + which)

    sibling = member(z_at, y_at, twin)
    across = member(z_at, over, core)
    ahead = [member(column(step), y_at, core) for step in range(side)]
    behind = [member(column(-step), y_at, core) for step in range(side)]
    following = (series, lax.rem(tm + 1, count))
    preceding = (series, lax.rem(tm + count - 1, count))

    loads = [
        pltpu.make_async_copy(source, target, load_sem.at[index])
        for index, (source, target) in enumerate(
            (
                (b_hbm, b_own),
                (f_hbm, f_own),
                (y_hbm, y_buf),
                (w_hbm, w_buf),
                (cb_hbm, cb_buf),
                (m_hbm, m_own),
                (v_hbm, v_own),
                (mask_hbm, mask_in),
                (dil_hbm, dil_ref),
            )
        )
    ]
    for load in loads:
        load.start()

    barrier = pltpu.get_barrier_semaphore()
    others = [(lax.rem(series + step, groups), tm) for step in range(1, groups)]
    greeted = ahead[1:] + [across, sibling] + others
    for device in greeted:
        pl.semaphore_signal(barrier, inc=1, device_id=device, device_id_type=MESH)

    @pl.when(tm > 0)
    def _():
        pl.semaphore_signal(barrier, inc=1, device_id=preceding, device_id_type=MESH)

    loads[1].wait()
    f_buf[z_at, y_at, core] = f_own[...].astype(BF16)
    loads[0].wait()
    x_buf[series] = b_own[...].astype(BF16)
    gx[...] = jnp.zeros_like(gx)
    pl.semaphore_wait(barrier, len(greeted) + jnp.where(tm < count - 1, 1, 0))

    def remote(source, target, send, recv, device):
        return pltpu.make_async_remote_copy(
            src_ref=source,
            dst_ref=target,
            send_sem=send,
            recv_sem=recv,
            device_id=device,
            device_id_type=MESH,
        )

    pending = []

    def send(copy):
        copy.start()
        pending.append(copy)

    def same(ref, sends, recvs, index, device):
        return remote(ref, ref, sends.at[index], recvs.at[index], device)

    def z_arrival(step):
        ref = f_buf.at[column(-step), y_at, core]
        same(ref, z_send, z_recv, step - 1, ahead[step]).wait_recv()
        pass_on(step)

    def pass_on(step):
        ref = f_buf.at[column(-step), y_at, core]
        send(same(ref, y_send, y_recv, step, across))
        send(same(ref, pair_send, pair_recv, (step, 0), sibling))

    def y_arrival(step):
        ref = f_buf.at[column(-step), over, core]
        same(ref, y_send, y_recv, step, across).wait_recv()
        send(same(ref, pair_send, pair_recv, (step, 1), sibling))

    for step in range(1, groups):
        send(
            remote(
                x_buf.at[series],
                x_buf.at[series],
                x_send.at[step - 1],
                x_recv.at[step - 1],
                others[step - 1],
            )
        )
    for step in range(1, side):
        ref = f_buf.at[z_at, y_at, core]
        send(same(ref, z_send, z_recv, step - 1, ahead[step]))
        if step == 1:
            pass_on(0)

    for step in range(1, groups):
        origin = lax.rem(series + groups - step, groups)
        remote(
            x_buf.at[origin],
            x_buf.at[origin],
            x_send.at[step - 1],
            x_recv.at[step - 1],
            others[step - 1],
        ).wait_recv()
    rim_copy = remote(
        x_buf.at[:, :, pl.ds(width - REACH, REACH)],
        rim,
        rim_sem.at[0],
        rim_sem.at[1],
        following,
    )

    @pl.when(tm < count - 1)
    def _():
        rim_copy.start()

    x_now = x_buf[...].reshape(K, width)
    xt_buf[...] = x_now.astype(F32).T.astype(BF16)
    loads[2].wait()
    loads[7].wait()
    mask_ref[...] = mask_in[...].astype(F32).T

    band = min(2 * rows, 2 * TILE)

    def compute(z, y):
        first = (4 * z + 2 * y) * rows
        f_now = f_buf[z, y].reshape(2 * rows, K)
        x_full = x_buf[...].reshape(K, width)
        parts = []
        for start in range(0, 2 * rows, band):
            pred = jnp.dot(f_now[start : start + band], x_full, preferred_element_type=F32)
            for inner in range(0, band, TILE):
                at = pl.multiple_of(first + start + inner, TILE)
                y_now = y_buf[pl.ds(at, TILE), :].astype(F32)
                flags = mask_ref[pl.ds(at // TILE, 1), :]
                seen = jnp.concatenate(
                    [
                        jnp.broadcast_to(flags[:, column : column + 1], (1, TILE))
                        for column in range(width // TILE)
                    ],
                    axis=1,
                )
                parts.append((seen * (y_now - pred[inner : inner + TILE])).astype(BF16))
        rb = jnp.concatenate(parts, axis=0) if len(parts) > 1 else parts[0]
        gx[...] += lax.dot_general(
            f_now, rb, (((0,), (0,)), ((), ())), preferred_element_type=F32
        )
        return jnp.dot(rb, xt_buf[...], preferred_element_type=F32)

    def give_copy(step, row):
        index = (step, row)
        return remote(
            g_give.at[index], g_take.at[index], give_send.at[index], give_recv.at[index], sibling
        )

    def block(step, row):
        z, y = column(-step), over if row else y_at
        same(f_buf.at[z, y, twin], pair_send, pair_recv, (step, row), sibling).wait_recv()
        g_both[...] = compute(z, y).reshape(2, rows, K)
        g_give[step, row] = g_both[twin].astype(BF16)
        send(give_copy(step, row))
        g_own[step, row] = g_both[core]

    def pair_total(step, row):
        give_copy(step, row).wait_recv()
        return g_own[step, row] + g_take[step, row].astype(F32)

    def y_sum_copy(step):
        return remote(
            y_sum_out.at[step],
            y_sum_in.at[step],
            y_sum_send.at[step],
            y_sum_recv.at[step],
            across,
        )

    def y_send_sum(step):
        y_sum_out[step] = pair_total(step, 1).astype(BF16)
        send(y_sum_copy(step))

    def chip_total(step):
        total = pair_total(step, 0)
        y_sum_copy(step).wait_recv()
        return total + y_sum_in[step].astype(F32)

    def z_sum_copy(step):
        return remote(
            z_sum_out.at[step - 1],
            z_sum_in.at[step - 1],
            z_sum_send.at[step - 1],
            z_sum_recv.at[step - 1],
            behind[step],
        )

    def z_send_sum(step):
        z_sum_out[step - 1] = chip_total(step).astype(BF16)
        send(z_sum_copy(step))

    block(0, 0)
    z_arrival(1)
    y_arrival(0)
    if side > 2:
        z_arrival(2)
    for step in range(1, side):
        block(step, 0)
        if step + 2 < side:
            z_arrival(step + 2)
        y_arrival(step)
    order = list(range(1, side)) + [0]
    for turn, step in enumerate(order):
        block(step, 1)
        if turn >= 1:
            y_send_sum(order[turn - 1])
        if turn >= 2:
            z_send_sum(order[turn - 2])

    for step in range(1, groups):
        target = lax.rem(series + step, groups)
        rows_of = pl.ds(pl.multiple_of(target * part, part), part)
        gx_out[step - 1] = gx[rows_of, :].astype(BF16)
        send(
            remote(
                gx_out.at[step - 1],
                gx_in.at[step - 1],
                gx_send.at[step - 1],
                gx_recv.at[step - 1],
                others[step - 1],
            )
        )

    span = width + REACH
    @pl.when(tm > 0)
    def _():
        rim_copy.wait_recv()

    loads[3].wait()
    loads[4].wait()
    loads[8].wait()
    places = tm * width - REACH + lax.broadcasted_iota(jnp.int32, (K, span), 1)
    inside = places >= 0
    hidden = jnp.concatenate([rim[...].reshape(K, REACH), x_now], axis=1).astype(F32)
    hidden = jnp.where(inside, hidden, 0.0)

    def conv_layer(hidden, layer):
        hb = hidden.astype(BF16)
        past = pltpu.roll(hb.astype(F32), dil_ref[layer], 1).astype(BF16)
        z_val = jnp.dot(w_buf[layer, 0], past, preferred_element_type=F32)
        z_val = z_val + jnp.dot(w_buf[layer, 1], hb, preferred_element_type=F32)
        z_val = z_val + cb_buf[layer][:, None]
        return jnp.where(inside, hidden + jnp.maximum(z_val, 0.0), 0.0)

    for layer in range(LAYERS):
        if layer == 1:
            y_send_sum(0)
        if layer == 2:
            z_send_sum(side - 1)
        hidden = conv_layer(hidden, layer)
    h_buf[...] = hidden[:, REACH:]

    own_rows = pl.ds(pl.multiple_of(series * part, part), part)
    grad_x = gx[own_rows, :]
    for step in range(1, groups):
        remote(
            gx_out.at[step - 1],
            gx_in.at[step - 1],
            gx_send.at[step - 1],
            gx_recv.at[step - 1],
            others[step - 1],
        ).wait_recv()
        grad_x = grad_x + gx_in[step - 1].astype(F32)
    grad_x = -grad_x * math.sqrt(K / total_series)
    basis = b_own[...]
    b_out[...] = basis - 0.5 * (grad_x + (basis - h_buf[own_rows, :]))
    stores = [
        pltpu.make_async_copy(source, target, load_sem.at[len(loads) + index])
        for index, (source, target) in enumerate(
            ((f_out, f_end), (m_out, m_end), (v_out, v_end), (b_out, b_end))
        )
    ]
    stores[3].start()

    loads[5].wait()
    loads[6].wait()
    scale_f = 1.0 / math.sqrt(total_time)
    value = chip_total(0)
    for step in range(1, side):
        z_sum_copy(step).wait_recv()
        value = value + z_sum_in[step - 1].astype(F32)
    grad_f = -value * scale_f
    m_new = 0.9 * m_own[...] + 0.1 * grad_f
    v_new = 0.999 * v_own[...] + 0.001 * grad_f * grad_f
    m_hat = m_new / (1.0 - 0.9**10)
    v_hat = v_new / (1.0 - 0.999**10)
    f_out[...] = f_own[...] - 0.01 * m_hat / (jnp.sqrt(v_hat) + 1e-08)
    m_out[...] = m_new
    v_out[...] = v_new
    for store in stores[:3]:
        store.start()

    for copy in pending:
        copy.wait_send()

    @pl.when(tm < count - 1)
    def _():
        rim_copy.wait_send()

    for store in stores:
        store.wait()


def hand_out(*refs):
    sources, targets, held, sem = refs[:4], refs[4:8], refs[8:12], refs[12]
    loads = [pltpu.make_async_copy(sources[i], held[i], sem.at[i]) for i in range(4)]
    stores = [pltpu.make_async_copy(held[i], targets[i], sem.at[4 + i]) for i in range(4)]
    for load in loads:
        load.start()
    for load, store in zip(loads, stores):
        load.wait()
        store.start()
    for store in stores:
        store.wait()


def on_device(count, groups, y_obs, tile_mask, factors, adam_m, adam_v, basis, dilations, conv_w, conv_b):
    rows = factors.shape[0]
    part, width = basis.shape
    side = count // 4
    dma = pltpu.SemaphoreType.DMA
    hbm = pl.BlockSpec(memory_space=pltpu.HBM)
    work = y_obs.shape[0] * width * K * 6
    results = pl.pallas_call(
        functools.partial(kernel, count, groups),
        out_shape=(
            jax.ShapeDtypeStruct(factors.shape, F32),
            jax.ShapeDtypeStruct(factors.shape, F32),
            jax.ShapeDtypeStruct(factors.shape, F32),
            jax.ShapeDtypeStruct(basis.shape, F32),
        ),
        in_specs=[hbm] * 9,
        out_specs=(hbm,) * 4,
        scratch_shapes=[
            pltpu.VMEM(factors.shape, F32),
            pltpu.VMEM(factors.shape, F32),
            pltpu.VMEM(factors.shape, F32),
            pltpu.VMEM(basis.shape, F32),
            pltpu.VMEM(y_obs.shape, BF16),
            pltpu.VMEM(tile_mask.shape[::-1], jnp.int32),
            pltpu.VMEM(tile_mask.shape, F32),
            pltpu.SMEM(dilations.shape, jnp.int32),
            pltpu.VMEM(factors.shape, F32),
            pltpu.VMEM(factors.shape, F32),
            pltpu.VMEM(factors.shape, F32),
            pltpu.VMEM(basis.shape, F32),
            pltpu.VMEM(conv_w.shape, BF16),
            pltpu.VMEM(conv_b.shape, F32),
            pltpu.VMEM((side, 2, 2, rows, K), BF16),
            pltpu.VMEM((groups, part, width), BF16),
            pltpu.VMEM((width, K), BF16),
            pltpu.VMEM((groups, part, REACH), BF16),
            pltpu.VMEM((2, rows, K), F32),
            pltpu.VMEM((side, 2, rows, K), F32),
            pltpu.VMEM((side, 2, rows, K), BF16),
            pltpu.VMEM((side, 2, rows, K), BF16),
            pltpu.VMEM((side, rows, K), BF16),
            pltpu.VMEM((side, rows, K), BF16),
            pltpu.VMEM((side - 1, rows, K), BF16),
            pltpu.VMEM((side - 1, rows, K), BF16),
            pltpu.VMEM((K, width), F32),
            pltpu.VMEM((max(groups - 1, 1), part, width), BF16),
            pltpu.VMEM((max(groups - 1, 1), part, width), BF16),
            pltpu.VMEM((K, width), F32),
            dma((13,)),
            dma((side - 1,)),
            dma((side - 1,)),
            dma((side,)),
            dma((side,)),
            dma((side, 2)),
            dma((side, 2)),
            dma((max(groups - 1, 1),)),
            dma((max(groups - 1, 1),)),
            dma((2,)),
            dma((side, 2)),
            dma((side, 2)),
            dma((side,)),
            dma((side,)),
            dma((side - 1,)),
            dma((side - 1,)),
            dma((max(groups - 1, 1),)),
            dma((max(groups - 1, 1),)),
        ],
        compiler_params=pltpu.CompilerParams(
            collective_id=0, has_side_effects=True, vmem_limit_bytes=60 * 2**20
        ),
        cost_estimate=pl.CostEstimate(
            flops=work, bytes_accessed=2 * y_obs.size, transcendentals=factors.size
        ),
    )(y_obs, tile_mask.T, factors, adam_m, adam_v, basis, dilations, conv_w, conv_b)
    return pl.pallas_call(
        hand_out,
        out_shape=tuple(jax.ShapeDtypeStruct(result.shape, F32) for result in results),
        in_specs=[hbm] * 4,
        out_specs=(hbm,) * 4,
        scratch_shapes=[pltpu.VMEM(result.shape, F32) for result in results] + [dma((8,))],
        compiler_params=pltpu.CompilerParams(vmem_limit_bytes=60 * 2**20),
    )(*results)


def solution(mesh):
    return jax.shard_map(
        functools.partial(on_device, mesh.shape["tm"], mesh.shape["series"]),
        mesh=mesh,
        in_specs=(
            P("series", "tm"),
            P("series", "tm"),
            P(("series", "tm"), None),
            P(("series", "tm"), None),
            P(("series", "tm"), None),
            P("series", "tm"),
            P(),
            P(),
            P(),
        ),
        out_specs=(
            P(("series", "tm"), None),
            P(("series", "tm"), None),
            P(("series", "tm"), None),
            P("series", "tm"),
        ),
        check_vma=False,
    )
```

```python
import functools
import math

import jax
import jax.numpy as jnp
from jax import lax
from jax.experimental import pallas as pl
from jax.experimental.pallas import tpu as pltpu
from jax.sharding import PartitionSpec as P

K = 128
TILE = 128
LAYERS = 4
D_MAX = 32
REACH = LAYERS * D_MAX
MESH = pl.DeviceIdType.MESH
F32 = jnp.float32
BF16 = jnp.bfloat16


def kernel(
    count,
    groups,
    y_hbm,
    mask_hbm,
    f_hbm,
    m_hbm,
    v_hbm,
    b_hbm,
    dil_hbm,
    w_hbm,
    cb_hbm,
    f_end,
    m_end,
    v_end,
    b_end,
    f_out,
    m_out,
    v_out,
    b_out,
    y_buf,
    mask_in,
    mask_ref,
    dil_ref,
    f_own,
    m_own,
    v_own,
    b_own,
    w_buf,
    cb_buf,
    f_buf,
    x_buf,
    xt_buf,
    rim,
    g_both,
    g_own,
    g_give,
    g_take,
    y_sum_out,
    y_sum_in,
    z_sum_out,
    z_sum_in,
    gx,
    gx_out,
    gx_in,
    h_buf,
    load_sem,
    z_send,
    z_recv,
    y_send,
    y_recv,
    pair_send,
    pair_recv,
    x_send,
    x_recv,
    rim_sem,
    give_send,
    give_recv,
    y_sum_send,
    y_sum_recv,
    z_sum_send,
    z_sum_recv,
    gx_send,
    gx_recv,
):
    side = count // 4
    rows = f_own.shape[0]
    part, width = b_own.shape
    total_time = width * count
    total_series = rows * count * groups

    series = lax.axis_index("series")
    tm = lax.axis_index("tm")
    core = lax.rem(tm, 2)
    twin = 1 - core
    y_at = lax.rem(tm // 2, 2)
    over = 1 - y_at
    z_at = tm // 4

    def column(step):
        return lax.rem(z_at + side + step, side)

    def member(z, y, which):
        return (series, 4 * z + 2 * y + which)

    sibling = member(z_at, y_at, twin)
    across = member(z_at, over, core)
    ahead = [member(column(step), y_at, core) for step in range(side)]
    following = (series, lax.rem(tm + 1, count))
    preceding = (series, lax.rem(tm + count - 1, count))

    loads = [
        pltpu.make_async_copy(source, target, load_sem.at[index])
        for index, (source, target) in enumerate(
            (
                (b_hbm, b_own),
                (f_hbm, f_own),
                (y_hbm, y_buf),
                (w_hbm, w_buf),
                (cb_hbm, cb_buf),
                (m_hbm, m_own),
                (v_hbm, v_own),
                (mask_hbm, mask_in),
                (dil_hbm, dil_ref),
            )
        )
    ]
    for load in loads:
        load.start()

    barrier = pltpu.get_barrier_semaphore()
    others = [(lax.rem(series + step, groups), tm) for step in range(1, groups)]
    greeted = ahead[1:] + [across, sibling] + others
    for device in greeted:
        pl.semaphore_signal(barrier, inc=1, device_id=device, device_id_type=MESH)

    @pl.when(tm > 0)
    def _():
        pl.semaphore_signal(barrier, inc=1, device_id=preceding, device_id_type=MESH)

    loads[1].wait()
    f_buf[z_at, y_at, core] = f_own[...].astype(BF16)
    loads[0].wait()
    x_buf[series] = b_own[...].astype(BF16)
    gx[...] = jnp.zeros_like(gx)
    pl.semaphore_wait(barrier, len(greeted) + jnp.where(tm < count - 1, 1, 0))

    def remote(source, target, send, recv, device):
        return pltpu.make_async_remote_copy(
            src_ref=source,
            dst_ref=target,
            send_sem=send,
            recv_sem=recv,
            device_id=device,
            device_id_type=MESH,
        )

    pending = []

    def send(copy):
        copy.start()
        pending.append(copy)

    def same(ref, sends, recvs, index, device):
        return remote(ref, ref, sends.at[index], recvs.at[index], device)

    def z_arrival(step):
        ref = f_buf.at[column(-step), y_at, core]
        same(ref, z_send, z_recv, step - 1, across).wait_recv()
        pass_on(step)

    def pass_on(step):
        ref = f_buf.at[column(-step), y_at, core]
        same(ref, y_send, y_recv, step, across).start()
        same(ref, pair_send, pair_recv, (step, 0), sibling).start()

    def y_arrival(step):
        ref = f_buf.at[column(-step), over, core]
        same(ref, y_send, y_recv, step, across).wait_recv()
        same(ref, pair_send, pair_recv, (step, 1), sibling).start()

    for step in range(1, groups):
        send(
            remote(
                x_buf.at[series],
                x_buf.at[series],
                x_send.at[step - 1],
                x_recv.at[step - 1],
                others[step - 1],
            )
        )
    for step in range(1, side):
        ref = f_buf.at[z_at, y_at, core]
        send(same(ref, z_send, z_recv, step - 1, ahead[step]))
        if step == 1:
            pass_on(0)

    for step in range(1, groups):
        origin = lax.rem(series + groups - step, groups)
        remote(
            x_buf.at[origin],
            x_buf.at[origin],
            x_send.at[step - 1],
            x_recv.at[step - 1],
            others[step - 1],
        ).wait_recv()
    rim_copy = remote(
        x_buf.at[:, :, pl.ds(width - REACH, REACH)],
        rim,
        rim_sem.at[0],
        rim_sem.at[1],
        following,
    )

    @pl.when(tm < count - 1)
    def _():
        rim_copy.start()

    x_now = x_buf[...].reshape(K, width)
    xt_buf[...] = x_now.astype(F32).T.astype(BF16)
    loads[2].wait()
    loads[7].wait()
    mask_ref[...] = mask_in[...].astype(F32).T

    band = min(2 * rows, 2 * TILE)

    def compute(z, y):
        first = (4 * z + 2 * y) * rows
        f_now = f_buf[z, y].reshape(2 * rows, K)
        x_full = x_buf[...].reshape(K, width)
        parts = []
        for start in range(0, 2 * rows, band):
            pred = jnp.dot(f_now[start : start + band], x_full, preferred_element_type=F32)
            for inner in range(0, band, TILE):
                at = pl.multiple_of(first + start + inner, TILE)
                y_now = y_buf[pl.ds(at, TILE), :].astype(F32)
                flags = mask_ref[pl.ds(at // TILE, 1), :]
                seen = jnp.concatenate(
                    [
                        jnp.broadcast_to(flags[:, column : column + 1], (1, TILE))
                        for column in range(width // TILE)
                    ],
                    axis=1,
                )
                parts.append((seen * (y_now - pred[inner : inner + TILE])).astype(BF16))
        rb = jnp.concatenate(parts, axis=0) if len(parts) > 1 else parts[0]
        gx[...] += lax.dot_general(
            f_now, rb, (((0,), (0,)), ((), ())), preferred_element_type=F32
        )
        return jnp.dot(rb, xt_buf[...], preferred_element_type=F32)

    def give_copy(step, row):
        index = (step, row)
        return remote(
            g_give.at[index], g_take.at[index], give_send.at[index], give_recv.at[index], sibling
        )

    def block(step, row):
        z, y = column(-step), y_at + row * (over - y_at)
        same(f_buf.at[z, y, twin], pair_send, pair_recv, (step, row), sibling).wait_recv()
        g_both[...] = compute(z, y).reshape(2, rows, K)
        g_give[step, row] = g_both[twin].astype(BF16)
        give_copy(step, row).start()
        g_own[step, row] = g_both[core]

    def pair_total(step, row):
        give_copy(step, row).wait_recv()
        return g_own[step, row] + g_take[step, row].astype(F32)

    def y_sum_copy(step):
        return remote(
            y_sum_out.at[step],
            y_sum_in.at[step],
            y_sum_send.at[step],
            y_sum_recv.at[step],
            across,
        )

    def y_send_sum(step):
        y_sum_out[step] = pair_total(step, 1).astype(BF16)
        y_sum_copy(step).start()

    def chip_total(step):
        total = pair_total(step, 0)
        y_sum_copy(step).wait_recv()
        return total + y_sum_in[step].astype(F32)

    def z_sum_copy(step):
        return remote(
            z_sum_out.at[step - 1],
            z_sum_in.at[step - 1],
            z_sum_send.at[step - 1],
            z_sum_recv.at[step - 1],
            member(column(-step), y_at, core),
        )

    def z_send_sum(step):
        z_sum_out[step - 1] = chip_total(step).astype(BF16)
        z_sum_copy(step).start()

    @pl.loop(0, 2 * side)
    def _(turn):
        row = turn // side
        block(lax.rem(turn + row, side), row)

        @pl.when(turn == 0)
        def _():
            z_arrival(1)

        @pl.when(turn + 2 < side)
        def _():
            z_arrival(turn + 2)

        @pl.when(turn < side)
        def _():
            y_arrival(turn)

        @pl.when(turn > side)
        def _():
            y_send_sum(turn - side)

        @pl.when(turn > side + 1)
        def _():
            z_send_sum(turn - side - 1)

    for step in range(1, groups):
        target = lax.rem(series + step, groups)
        rows_of = pl.ds(pl.multiple_of(target * part, part), part)
        gx_out[step - 1] = gx[rows_of, :].astype(BF16)
        send(
            remote(
                gx_out.at[step - 1],
                gx_in.at[step - 1],
                gx_send.at[step - 1],
                gx_recv.at[step - 1],
                others[step - 1],
            )
        )

    span = width + REACH
    @pl.when(tm > 0)
    def _():
        rim_copy.wait_recv()

    loads[3].wait()
    loads[4].wait()
    loads[8].wait()
    places = tm * width - REACH + lax.broadcasted_iota(jnp.int32, (K, span), 1)
    inside = places >= 0
    hidden = jnp.concatenate([rim[...].reshape(K, REACH), x_now], axis=1).astype(F32)
    hidden = jnp.where(inside, hidden, 0.0)

    def conv_layer(hidden, layer):
        hb = hidden.astype(BF16)
        past = pltpu.roll(hb.astype(F32), dil_ref[layer], 1).astype(BF16)
        z_val = jnp.dot(w_buf[layer, 0], past, preferred_element_type=F32)
        z_val = z_val + jnp.dot(w_buf[layer, 1], hb, preferred_element_type=F32)
        z_val = z_val + cb_buf[layer][:, None]
        return jnp.where(inside, hidden + jnp.maximum(z_val, 0.0), 0.0)

    for layer in range(LAYERS):
        if layer == 1:
            y_send_sum(0)
        if layer == 2:
            z_send_sum(side - 1)
        hidden = conv_layer(hidden, layer)
    h_buf[...] = hidden[:, REACH:]

    own_rows = pl.ds(pl.multiple_of(series * part, part), part)
    grad_x = gx[own_rows, :]
    for step in range(1, groups):
        remote(
            gx_out.at[step - 1],
            gx_in.at[step - 1],
            gx_send.at[step - 1],
            gx_recv.at[step - 1],
            others[step - 1],
        ).wait_recv()
        grad_x = grad_x + gx_in[step - 1].astype(F32)
    grad_x = -grad_x * math.sqrt(K / total_series)
    basis = b_own[...]
    b_out[...] = basis - 0.5 * (grad_x + (basis - h_buf[own_rows, :]))
    stores = [
        pltpu.make_async_copy(source, target, load_sem.at[len(loads) + index])
        for index, (source, target) in enumerate(
            ((f_out, f_end), (m_out, m_end), (v_out, v_end), (b_out, b_end))
        )
    ]
    stores[3].start()

    loads[5].wait()
    loads[6].wait()
    scale_f = 1.0 / math.sqrt(total_time)
    value = chip_total(0)
    for step in range(1, side):
        z_sum_copy(step).wait_recv()
        value = value + z_sum_in[step - 1].astype(F32)
    grad_f = -value * scale_f
    m_new = 0.9 * m_own[...] + 0.1 * grad_f
    v_new = 0.999 * v_own[...] + 0.001 * grad_f * grad_f
    m_hat = m_new / (1.0 - 0.9**10)
    v_hat = v_new / (1.0 - 0.999**10)
    f_out[...] = f_own[...] - 0.01 * m_hat / (jnp.sqrt(v_hat) + 1e-08)
    m_out[...] = m_new
    v_out[...] = v_new
    for store in stores[:3]:
        store.start()

    for copy in pending:
        copy.wait_send()

    @pl.loop(0, side)
    def _(step):
        own = f_buf.at[column(-step), y_at, core]
        other = f_buf.at[column(-step), over, core]
        same(own, y_send, y_recv, step, across).wait_send()
        same(own, pair_send, pair_recv, (step, 0), sibling).wait_send()
        same(other, pair_send, pair_recv, (step, 1), sibling).wait_send()
        give_copy(step, 0).wait_send()
        give_copy(step, 1).wait_send()
        y_sum_copy(step).wait_send()

        @pl.when(step > 0)
        def _():
            z_sum_copy(step).wait_send()

    @pl.when(tm < count - 1)
    def _():
        rim_copy.wait_send()

    for store in stores:
        store.wait()


def hand_out(*refs):
    sources, targets, held, sem = refs[:4], refs[4:8], refs[8:12], refs[12]
    loads = [pltpu.make_async_copy(sources[i], held[i], sem.at[i]) for i in range(4)]
    stores = [pltpu.make_async_copy(held[i], targets[i], sem.at[4 + i]) for i in range(4)]
    for load in loads:
        load.start()
    for load, store in zip(loads, stores):
        load.wait()
        store.start()
    for store in stores:
        store.wait()


def on_device(count, groups, y_obs, tile_mask, factors, adam_m, adam_v, basis, dilations, conv_w, conv_b):
    rows = factors.shape[0]
    part, width = basis.shape
    side = count // 4
    dma = pltpu.SemaphoreType.DMA
    hbm = pl.BlockSpec(memory_space=pltpu.HBM)
    work = y_obs.shape[0] * width * K * 6
    results = pl.pallas_call(
        functools.partial(kernel, count, groups),
        out_shape=(
            jax.ShapeDtypeStruct(factors.shape, F32),
            jax.ShapeDtypeStruct(factors.shape, F32),
            jax.ShapeDtypeStruct(factors.shape, F32),
            jax.ShapeDtypeStruct(basis.shape, F32),
        ),
        in_specs=[hbm] * 9,
        out_specs=(hbm,) * 4,
        scratch_shapes=[
            pltpu.VMEM(factors.shape, F32),
            pltpu.VMEM(factors.shape, F32),
            pltpu.VMEM(factors.shape, F32),
            pltpu.VMEM(basis.shape, F32),
            pltpu.VMEM(y_obs.shape, BF16),
            pltpu.VMEM(tile_mask.shape[::-1], jnp.int32),
            pltpu.VMEM(tile_mask.shape, F32),
            pltpu.SMEM(dilations.shape, jnp.int32),
            pltpu.VMEM(factors.shape, F32),
            pltpu.VMEM(factors.shape, F32),
            pltpu.VMEM(factors.shape, F32),
            pltpu.VMEM(basis.shape, F32),
            pltpu.VMEM(conv_w.shape, BF16),
            pltpu.VMEM(conv_b.shape, F32),
            pltpu.VMEM((side, 2, 2, rows, K), BF16),
            pltpu.VMEM((groups, part, width), BF16),
            pltpu.VMEM((width, K), BF16),
            pltpu.VMEM((groups, part, REACH), BF16),
            pltpu.VMEM((2, rows, K), F32),
            pltpu.VMEM((side, 2, rows, K), F32),
            pltpu.VMEM((side, 2, rows, K), BF16),
            pltpu.VMEM((side, 2, rows, K), BF16),
            pltpu.VMEM((side, rows, K), BF16),
            pltpu.VMEM((side, rows, K), BF16),
            pltpu.VMEM((side - 1, rows, K), BF16),
            pltpu.VMEM((side - 1, rows, K), BF16),
            pltpu.VMEM((K, width), F32),
            pltpu.VMEM((max(groups - 1, 1), part, width), BF16),
            pltpu.VMEM((max(groups - 1, 1), part, width), BF16),
            pltpu.VMEM((K, width), F32),
            dma((13,)),
            dma((side - 1,)),
            dma((side - 1,)),
            dma((side,)),
            dma((side,)),
            dma((side, 2)),
            dma((side, 2)),
            dma((max(groups - 1, 1),)),
            dma((max(groups - 1, 1),)),
            dma((2,)),
            dma((side, 2)),
            dma((side, 2)),
            dma((side,)),
            dma((side,)),
            dma((side - 1,)),
            dma((side - 1,)),
            dma((max(groups - 1, 1),)),
            dma((max(groups - 1, 1),)),
        ],
        compiler_params=pltpu.CompilerParams(
            collective_id=0, has_side_effects=True, vmem_limit_bytes=60 * 2**20
        ),
        cost_estimate=pl.CostEstimate(
            flops=work, bytes_accessed=2 * y_obs.size, transcendentals=factors.size
        ),
    )(y_obs, tile_mask.T, factors, adam_m, adam_v, basis, dilations, conv_w, conv_b)
    return pl.pallas_call(
        hand_out,
        out_shape=tuple(jax.ShapeDtypeStruct(result.shape, F32) for result in results),
        in_specs=[hbm] * 4,
        out_specs=(hbm,) * 4,
        scratch_shapes=[pltpu.VMEM(result.shape, F32) for result in results] + [dma((8,))],
        compiler_params=pltpu.CompilerParams(vmem_limit_bytes=60 * 2**20),
    )(*results)


def solution(mesh):
    return jax.shard_map(
        functools.partial(on_device, mesh.shape["tm"], mesh.shape["series"]),
        mesh=mesh,
        in_specs=(
            P("series", "tm"),
            P("series", "tm"),
            P(("series", "tm"), None),
            P(("series", "tm"), None),
            P(("series", "tm"), None),
            P("series", "tm"),
            P(),
            P(),
            P(),
        ),
        out_specs=(
            P(("series", "tm"), None),
            P(("series", "tm"), None),
            P(("series", "tm"), None),
            P("series", "tm"),
        ),
        check_vma=False,
    )
```

```python
import functools
import math

import jax
import jax.numpy as jnp
from jax import lax
from jax.experimental import pallas as pl
from jax.experimental.pallas import tpu as pltpu
from jax.sharding import PartitionSpec as P

K = 128
TILE = 128
LAYERS = 4
D_MAX = 32
REACH = LAYERS * D_MAX
MESH = pl.DeviceIdType.MESH
F32 = jnp.float32
BF16 = jnp.bfloat16


def kernel(
    count,
    groups,
    y_hbm,
    mask_hbm,
    f_hbm,
    m_hbm,
    v_hbm,
    b_hbm,
    dil_hbm,
    w_hbm,
    cb_hbm,
    f_end,
    m_end,
    v_end,
    b_end,
    f_out,
    m_out,
    v_out,
    b_out,
    y_buf,
    mask_in,
    mask_ref,
    dil_ref,
    f_own,
    m_own,
    v_own,
    b_own,
    w_buf,
    cb_buf,
    f_buf,
    x_buf,
    xt_buf,
    rim,
    g_both,
    g_own,
    g_give,
    g_take,
    y_sum_out,
    y_sum_in,
    z_sum_out,
    z_sum_in,
    gx,
    gx_out,
    gx_in,
    h_buf,
    load_sem,
    z_send,
    z_recv,
    y_send,
    y_recv,
    pair_send,
    pair_recv,
    x_send,
    x_recv,
    rim_sem,
    give_send,
    give_recv,
    y_sum_send,
    y_sum_recv,
    z_sum_send,
    z_sum_recv,
    gx_send,
    gx_recv,
):
    side = count // 4
    rows = f_own.shape[0]
    part, width = b_own.shape
    total_time = width * count
    total_series = rows * count * groups

    series = lax.axis_index("series")
    tm = lax.axis_index("tm")
    core = lax.rem(tm, 2)
    twin = 1 - core
    y_at = lax.rem(tm // 2, 2)
    over = 1 - y_at
    z_at = tm // 4

    def column(step):
        return lax.rem(z_at + side + step, side)

    def member(z, y, which):
        return (series, 4 * z + 2 * y + which)

    sibling = member(z_at, y_at, twin)
    across = member(z_at, over, core)
    ahead = [member(column(step), y_at, core) for step in range(side)]
    following = (series, lax.rem(tm + 1, count))
    preceding = (series, lax.rem(tm + count - 1, count))

    loads = [
        pltpu.make_async_copy(source, target, load_sem.at[index])
        for index, (source, target) in enumerate(
            (
                (b_hbm, b_own),
                (f_hbm, f_own),
                (y_hbm, y_buf),
                (w_hbm, w_buf),
                (cb_hbm, cb_buf),
                (m_hbm, m_own),
                (v_hbm, v_own),
                (mask_hbm, mask_in),
                (dil_hbm, dil_ref),
            )
        )
    ]
    for load in loads[:2]:
        load.start()

    barrier = pltpu.get_barrier_semaphore()
    others = [(lax.rem(series + step, groups), tm) for step in range(1, groups)]
    greeted = ahead[1:] + [across, sibling] + others
    for device in greeted:
        pl.semaphore_signal(barrier, inc=1, device_id=device, device_id_type=MESH)

    @pl.when(tm > 0)
    def _():
        pl.semaphore_signal(barrier, inc=1, device_id=preceding, device_id_type=MESH)

    loads[1].wait()
    f_buf[z_at, y_at, core] = f_own[...].astype(BF16)
    loads[0].wait()
    x_buf[series] = b_own[...].astype(BF16)
    for load in loads[2:]:
        load.start()
    gx[...] = jnp.zeros_like(gx)
    pl.semaphore_wait(barrier, len(greeted) + jnp.where(tm < count - 1, 1, 0))

    def remote(source, target, send, recv, device):
        return pltpu.make_async_remote_copy(
            src_ref=source,
            dst_ref=target,
            send_sem=send,
            recv_sem=recv,
            device_id=device,
            device_id_type=MESH,
        )

    pending = []

    def send(copy):
        copy.start()
        pending.append(copy)

    def same(ref, sends, recvs, index, device):
        return remote(ref, ref, sends.at[index], recvs.at[index], device)

    def z_arrival(step):
        ref = f_buf.at[column(-step), y_at, core]
        same(ref, z_send, z_recv, step - 1, across).wait_recv()
        pass_on(step)

    def pass_on(step):
        ref = f_buf.at[column(-step), y_at, core]
        same(ref, y_send, y_recv, step, across).start()
        same(ref, pair_send, pair_recv, (step, 0), sibling).start()

    def y_arrival(step):
        ref = f_buf.at[column(-step), over, core]
        same(ref, y_send, y_recv, step, across).wait_recv()
        same(ref, pair_send, pair_recv, (step, 1), sibling).start()

    for step in range(1, groups):
        send(
            remote(
                x_buf.at[series],
                x_buf.at[series],
                x_send.at[step - 1],
                x_recv.at[step - 1],
                others[step - 1],
            )
        )
    for step in range(1, side):
        ref = f_buf.at[z_at, y_at, core]
        send(same(ref, z_send, z_recv, step - 1, ahead[step]))
        if step == 1:
            pass_on(0)

    for step in range(1, groups):
        origin = lax.rem(series + groups - step, groups)
        remote(
            x_buf.at[origin],
            x_buf.at[origin],
            x_send.at[step - 1],
            x_recv.at[step - 1],
            others[step - 1],
        ).wait_recv()
    rim_copy = remote(
        x_buf.at[:, :, pl.ds(width - REACH, REACH)],
        rim,
        rim_sem.at[0],
        rim_sem.at[1],
        following,
    )

    @pl.when(tm < count - 1)
    def _():
        rim_copy.start()

    x_now = x_buf[...].reshape(K, width)
    xt_buf[...] = x_now.astype(F32).T.astype(BF16)
    loads[2].wait()
    loads[7].wait()
    mask_ref[...] = mask_in[...].astype(F32).T

    band = min(2 * rows, 2 * TILE)

    def compute(z, y):
        first = (4 * z + 2 * y) * rows
        f_now = f_buf[z, y].reshape(2 * rows, K)
        x_full = x_buf[...].reshape(K, width)
        parts = []
        for start in range(0, 2 * rows, band):
            pred = jnp.dot(f_now[start : start + band], x_full, preferred_element_type=F32)
            for inner in range(0, band, TILE):
                at = pl.multiple_of(first + start + inner, TILE)
                y_now = y_buf[pl.ds(at, TILE), :].astype(F32)
                flags = mask_ref[pl.ds(at // TILE, 1), :]
                seen = jnp.concatenate(
                    [
                        jnp.broadcast_to(flags[:, column : column + 1], (1, TILE))
                        for column in range(width // TILE)
                    ],
                    axis=1,
                )
                parts.append((seen * (y_now - pred[inner : inner + TILE])).astype(BF16))
        rb = jnp.concatenate(parts, axis=0) if len(parts) > 1 else parts[0]
        gx[...] += lax.dot_general(
            f_now, rb, (((0,), (0,)), ((), ())), preferred_element_type=F32
        )
        return jnp.dot(rb, xt_buf[...], preferred_element_type=F32)

    def give_copy(step, row):
        index = (step, row)
        return remote(
            g_give.at[index], g_take.at[index], give_send.at[index], give_recv.at[index], sibling
        )

    def block(step, row):
        z, y = column(-step), y_at + row * (over - y_at)
        same(f_buf.at[z, y, twin], pair_send, pair_recv, (step, row), sibling).wait_recv()
        g_both[...] = compute(z, y).reshape(2, rows, K)
        g_give[step, row] = g_both[twin].astype(BF16)
        give_copy(step, row).start()
        g_own[step, row] = g_both[core]

    def pair_total(step, row):
        give_copy(step, row).wait_recv()
        return g_own[step, row] + g_take[step, row].astype(F32)

    def y_sum_copy(step):
        return remote(
            y_sum_out.at[step],
            y_sum_in.at[step],
            y_sum_send.at[step],
            y_sum_recv.at[step],
            across,
        )

    def y_send_sum(step):
        y_sum_out[step] = pair_total(step, 1).astype(BF16)
        y_sum_copy(step).start()

    def chip_total(step):
        total = pair_total(step, 0)
        y_sum_copy(step).wait_recv()
        return total + y_sum_in[step].astype(F32)

    def z_sum_copy(step):
        return remote(
            z_sum_out.at[step - 1],
            z_sum_in.at[step - 1],
            z_sum_send.at[step - 1],
            z_sum_recv.at[step - 1],
            member(column(-step), y_at, core),
        )

    def z_send_sum(step):
        z_sum_out[step - 1] = chip_total(step).astype(BF16)
        z_sum_copy(step).start()

    @pl.loop(0, 2 * side)
    def _(turn):
        row = turn // side
        block(lax.rem(turn + row, side), row)

        @pl.when(turn == 0)
        def _():
            z_arrival(1)

        @pl.when(turn + 2 < side)
        def _():
            z_arrival(turn + 2)

        @pl.when(turn < side)
        def _():
            y_arrival(turn)

        @pl.when(turn > side)
        def _():
            y_send_sum(turn - side)

        @pl.when(turn > side + 1)
        def _():
            z_send_sum(turn - side - 1)

    for step in range(1, groups):
        target = lax.rem(series + step, groups)
        rows_of = pl.ds(pl.multiple_of(target * part, part), part)
        gx_out[step - 1] = gx[rows_of, :].astype(BF16)
        send(
            remote(
                gx_out.at[step - 1],
                gx_in.at[step - 1],
                gx_send.at[step - 1],
                gx_recv.at[step - 1],
                others[step - 1],
            )
        )

    span = width + REACH
    @pl.when(tm > 0)
    def _():
        rim_copy.wait_recv()

    loads[3].wait()
    loads[4].wait()
    loads[8].wait()
    places = tm * width - REACH + lax.broadcasted_iota(jnp.int32, (K, span), 1)
    inside = places >= 0
    hidden = jnp.concatenate([rim[...].reshape(K, REACH), x_now], axis=1).astype(F32)
    hidden = jnp.where(inside, hidden, 0.0)

    def conv_layer(hidden, layer):
        hb = hidden.astype(BF16)
        past = pltpu.roll(hb.astype(F32), dil_ref[layer], 1).astype(BF16)
        z_val = jnp.dot(w_buf[layer, 0], past, preferred_element_type=F32)
        z_val = z_val + jnp.dot(w_buf[layer, 1], hb, preferred_element_type=F32)
        z_val = z_val + cb_buf[layer][:, None]
        return jnp.where(inside, hidden + jnp.maximum(z_val, 0.0), 0.0)

    for layer in range(LAYERS):
        if layer == 1:
            y_send_sum(0)
        if layer == 2:
            z_send_sum(side - 1)
        hidden = conv_layer(hidden, layer)
    h_buf[...] = hidden[:, REACH:]

    own_rows = pl.ds(pl.multiple_of(series * part, part), part)
    grad_x = gx[own_rows, :]
    for step in range(1, groups):
        remote(
            gx_out.at[step - 1],
            gx_in.at[step - 1],
            gx_send.at[step - 1],
            gx_recv.at[step - 1],
            others[step - 1],
        ).wait_recv()
        grad_x = grad_x + gx_in[step - 1].astype(F32)
    grad_x = -grad_x * math.sqrt(K / total_series)
    basis = b_own[...]
    b_out[...] = basis - 0.5 * (grad_x + (basis - h_buf[own_rows, :]))
    stores = [
        pltpu.make_async_copy(source, target, load_sem.at[len(loads) + index])
        for index, (source, target) in enumerate(
            ((f_out, f_end), (m_out, m_end), (v_out, v_end), (b_out, b_end))
        )
    ]
    stores[3].start()

    loads[5].wait()
    loads[6].wait()
    scale_f = 1.0 / math.sqrt(total_time)
    value = chip_total(0)
    for step in range(1, side):
        z_sum_copy(step).wait_recv()
        value = value + z_sum_in[step - 1].astype(F32)
    grad_f = -value * scale_f
    m_new = 0.9 * m_own[...] + 0.1 * grad_f
    v_new = 0.999 * v_own[...] + 0.001 * grad_f * grad_f
    m_hat = m_new / (1.0 - 0.9**10)
    v_hat = v_new / (1.0 - 0.999**10)
    f_out[...] = f_own[...] - 0.01 * m_hat / (jnp.sqrt(v_hat) + 1e-08)
    m_out[...] = m_new
    v_out[...] = v_new
    for store in stores[:3]:
        store.start()

    for copy in pending:
        copy.wait_send()

    @pl.loop(0, side)
    def _(step):
        own = f_buf.at[column(-step), y_at, core]
        other = f_buf.at[column(-step), over, core]
        same(own, y_send, y_recv, step, across).wait_send()
        same(own, pair_send, pair_recv, (step, 0), sibling).wait_send()
        same(other, pair_send, pair_recv, (step, 1), sibling).wait_send()
        give_copy(step, 0).wait_send()
        give_copy(step, 1).wait_send()
        y_sum_copy(step).wait_send()

        @pl.when(step > 0)
        def _():
            z_sum_copy(step).wait_send()

    @pl.when(tm < count - 1)
    def _():
        rim_copy.wait_send()

    for store in stores:
        store.wait()


def hand_out(*refs):
    sources, targets, held, sem = refs[:4], refs[4:8], refs[8:12], refs[12]
    loads = [pltpu.make_async_copy(sources[i], held[i], sem.at[i]) for i in range(4)]
    stores = [pltpu.make_async_copy(held[i], targets[i], sem.at[4 + i]) for i in range(4)]
    for load in loads:
        load.start()
    for load, store in zip(loads, stores):
        load.wait()
        store.start()
    for store in stores:
        store.wait()


def on_device(count, groups, y_obs, tile_mask, factors, adam_m, adam_v, basis, dilations, conv_w, conv_b):
    rows = factors.shape[0]
    part, width = basis.shape
    side = count // 4
    dma = pltpu.SemaphoreType.DMA
    hbm = pl.BlockSpec(memory_space=pltpu.HBM)
    work = y_obs.shape[0] * width * K * 6
    results = pl.pallas_call(
        functools.partial(kernel, count, groups),
        out_shape=(
            jax.ShapeDtypeStruct(factors.shape, F32),
            jax.ShapeDtypeStruct(factors.shape, F32),
            jax.ShapeDtypeStruct(factors.shape, F32),
            jax.ShapeDtypeStruct(basis.shape, F32),
        ),
        in_specs=[hbm] * 9,
        out_specs=(hbm,) * 4,
        scratch_shapes=[
            pltpu.VMEM(factors.shape, F32),
            pltpu.VMEM(factors.shape, F32),
            pltpu.VMEM(factors.shape, F32),
            pltpu.VMEM(basis.shape, F32),
            pltpu.VMEM(y_obs.shape, BF16),
            pltpu.VMEM(tile_mask.shape[::-1], jnp.int32),
            pltpu.VMEM(tile_mask.shape, F32),
            pltpu.SMEM(dilations.shape, jnp.int32),
            pltpu.VMEM(factors.shape, F32),
            pltpu.VMEM(factors.shape, F32),
            pltpu.VMEM(factors.shape, F32),
            pltpu.VMEM(basis.shape, F32),
            pltpu.VMEM(conv_w.shape, BF16),
            pltpu.VMEM(conv_b.shape, F32),
            pltpu.VMEM((side, 2, 2, rows, K), BF16),
            pltpu.VMEM((groups, part, width), BF16),
            pltpu.VMEM((width, K), BF16),
            pltpu.VMEM((groups, part, REACH), BF16),
            pltpu.VMEM((2, rows, K), F32),
            pltpu.VMEM((side, 2, rows, K), F32),
            pltpu.VMEM((side, 2, rows, K), BF16),
            pltpu.VMEM((side, 2, rows, K), BF16),
            pltpu.VMEM((side, rows, K), BF16),
            pltpu.VMEM((side, rows, K), BF16),
            pltpu.VMEM((side - 1, rows, K), BF16),
            pltpu.VMEM((side - 1, rows, K), BF16),
            pltpu.VMEM((K, width), F32),
            pltpu.VMEM((max(groups - 1, 1), part, width), BF16),
            pltpu.VMEM((max(groups - 1, 1), part, width), BF16),
            pltpu.VMEM((K, width), F32),
            dma((13,)),
            dma((side - 1,)),
            dma((side - 1,)),
            dma((side,)),
            dma((side,)),
            dma((side, 2)),
            dma((side, 2)),
            dma((max(groups - 1, 1),)),
            dma((max(groups - 1, 1),)),
            dma((2,)),
            dma((side, 2)),
            dma((side, 2)),
            dma((side,)),
            dma((side,)),
            dma((side - 1,)),
            dma((side - 1,)),
            dma((max(groups - 1, 1),)),
            dma((max(groups - 1, 1),)),
        ],
        compiler_params=pltpu.CompilerParams(
            collective_id=0, has_side_effects=True, vmem_limit_bytes=60 * 2**20
        ),
        cost_estimate=pl.CostEstimate(
            flops=work, bytes_accessed=2 * y_obs.size, transcendentals=factors.size
        ),
    )(y_obs, tile_mask.T, factors, adam_m, adam_v, basis, dilations, conv_w, conv_b)
    return pl.pallas_call(
        hand_out,
        out_shape=tuple(jax.ShapeDtypeStruct(result.shape, F32) for result in results),
        in_specs=[hbm] * 4,
        out_specs=(hbm,) * 4,
        scratch_shapes=[pltpu.VMEM(result.shape, F32) for result in results] + [dma((8,))],
        compiler_params=pltpu.CompilerParams(vmem_limit_bytes=60 * 2**20),
    )(*results)


def solution(mesh):
    return jax.shard_map(
        functools.partial(on_device, mesh.shape["tm"], mesh.shape["series"]),
        mesh=mesh,
        in_specs=(
            P("series", "tm"),
            P("series", "tm"),
            P(("series", "tm"), None),
            P(("series", "tm"), None),
            P(("series", "tm"), None),
            P("series", "tm"),
            P(),
            P(),
            P(),
        ),
        out_specs=(
            P(("series", "tm"), None),
            P(("series", "tm"), None),
            P(("series", "tm"), None),
            P("series", "tm"),
        ),
        check_vma=False,
    )
```
